32 devices in a mesh: member: 2 (over x), horiz: 16 (over z, y, core).
Axes of the slice: x: 2, y: 2, z: 4, core: 2. Of those that a mesh axis runs over, the one named last changes fastest.
Arguments:
- perturbation: float32 [16, 80, 4, 1920], P('member', 'horiz'), parts along dimension 0, may hold values from -36 to 36
- base_state: float32 [8, 80, 4, 1920], P(None, 'horiz'), may hold values from -6 to 6
- target_state: float32 [8, 80, 4, 1920], P(None, 'horiz'), may hold values from -6 to 6
- cost_weight: float32 [80, 1920], P('horiz'), may hold values from 0.5 to 6
- diffusivity: float32 [80, 1920], P('horiz'), may hold values from 0.04 to 0.2
- chan_mix: float32 [8, 4, 4], replicated, may hold values from -3 to 3
- coupler_mix: float32 [4, 4], replicated, may hold values from -3 to 3
- owner_mix: float32 [16, 80, 80], P('horiz'), may hold values from -0.625 to 0.625
- air_temp: float32 [2, 16, 80, 128], P(None, 'horiz'), may hold values from -6 to 6
- wind_speed: float32 [2, 16, 80, 128], P(None, 'horiz'), may hold values from 2 to 12
- wet_list: int32 [16, 75], P('horiz'), may hold values from -1 to 74, as said below
- wet_owner: int32 [16, 75], P('horiz'), may hold values from -1 to 15, as said below
- remap_src: int32 [240], P('horiz'), may hold values from 0 to 79, as said below
- remap_tgt: int32 [240], P('horiz'), may hold values from 0 to 31, as said below
- remap_weight: float32 [240], P('horiz'), may hold values from 0.2 to 0.8
Outputs:
- new_perturbation: float32 [16, 80, 4, 1920], P('member', 'horiz'), parts along dimension 0
The draws below stay inside these ranges and needn't reach their ends.
There are 2 independent parts, one for each index of `member`. The reference program is written for one: setup_inputs(seed, part) draws one part's arguments, and reference() takes and returns one part's arrays. A program takes and returns all parts, laid end to end along the dimension named above; an argument that names none is the same for every part. Nothing has to cross between parts.
Inputs may be any that keep to these rules, and one draw needn't show every extreme that they name: Each row of wet_list names distinct tiles, valid entries first and -1 after them; wet_owner is -1 exactly where wet_list is. Every device lists at least 37 wet tiles and some device lists all 75. Within one device's list no owner appears more than 5 times, and some owner appears exactly 5 times in every device's list. `wet_owner`: see wet_list. `remap_src`: the source row of each entry is one of the rows of the device that holds the entry. `remap_tgt`: each entry's latitude row differs from (2 times its source row) // 5 by at most 1.
All inputs are finite; a program needn't handle non-finite values.
Results may differ from the reference program's by a relative error of at most 0.0001.
Values sent between devices are 32-bit elements; how exact they have to be, the bound alone decides.
A program may use at most 64 MiB of HBM per device.

```python
import math
import jax
import jax.numpy as jnp
from jax import lax

LEV = 8
TILE = 128
TPR = 15
STEPS = 2
ROWS_DEV = 5
NLON = 1920
TILES_DEV = 75
NY = 80
NLAT = 32
CAP = 5
E_DEV = 15
NREMAP = 240
N_HORIZ = 16


def wet_tables(key):
    base_key = jax.random.fold_in(key, 7)
    key_count, key_full, key_hot, key_tiles, key_slots = jax.random.split(base_key, 5)
    counts = jax.random.randint(key_count, (N_HORIZ,), TILES_DEV // 2, TILES_DEV + 1)
    full_device = jax.random.randint(key_full, (), 0, N_HORIZ)
    counts = jnp.where(jnp.arange(N_HORIZ) == full_device, TILES_DEV, counts)
    hot_owner = jax.random.randint(key_hot, (), 0, N_HORIZ)
    slot_total = N_HORIZ * CAP

    def one_device(device):
        tile_order = jax.random.permutation(jax.random.fold_in(key_tiles, device), TILES_DEV)
        others = jax.random.permutation(jax.random.fold_in(key_slots, device), slot_total - CAP)
        others = jnp.where(others >= hot_owner * CAP, others + CAP, others)
        slot_order = jnp.concatenate([hot_owner * CAP + jnp.arange(CAP), others])[:TILES_DEV]
        owners = slot_order // CAP
        live = jnp.arange(TILES_DEV) < counts[device]
        return (jnp.where(live, tile_order, -1), jnp.where(live, owners, -1))
    wet_rows, owner_rows = jax.vmap(one_device)(jnp.arange(N_HORIZ))
    return (wet_rows.astype(jnp.int32), owner_rows.astype(jnp.int32))


def draw_wet_list(key, part):
    return wet_tables(key)[0]


def draw_wet_owner(key, part):
    return wet_tables(key)[1]


def remap_tables(key):
    base_key = jax.random.fold_in(key, 11)
    key_row, key_near = jax.random.split(base_key, 2)
    entry_total = N_HORIZ * E_DEV
    entry_index = jnp.arange(entry_total, dtype=jnp.int32)
    holder = entry_index // E_DEV
    local_row = jax.random.randint(key_row, (entry_total,), 0, ROWS_DEV)
    source = holder * ROWS_DEV + local_row
    target = jnp.clip(source * 2 // 5 + jax.random.randint(key_near, (entry_total,), -1, 2), 0, NLAT - 1)
    return (source.astype(jnp.int32), target.astype(jnp.int32))


def draw_remap_src(key, part):
    return remap_tables(key)[0]


def draw_remap_tgt(key, part):
    return remap_tables(key)[1]


def draw_perturbation(key, part):
    key_noise, key_rows, key_cols = jax.random.split(key, 3)
    shape = (LEV, NY, 4, NLON)
    noise = jnp.clip(jax.random.normal(key_noise, shape, jnp.float32), -6.0, 6.0)
    rise = 3.0 ** (jnp.arange(NY).astype(jnp.float32) / (NY - 1))
    row_scale = rise * 10.0 ** jax.random.uniform(key_rows, (NY,), jnp.float32)
    col_scale = 10.0 ** jax.random.uniform(key_cols, (NLON,), jnp.float32)
    return 0.02 * noise * row_scale[None, :, None, None] * col_scale[None, None, None, :]


def draw_cost_weight(key, part):
    rise = 3.0 ** (jnp.arange(NY).astype(jnp.float32) / (NY - 1))
    factor = 2.0 ** jax.random.uniform(key, (NY, NLON), jnp.float32, -1.0, 1.0)
    return rise[:, None] * factor


def block_scale(rng, dims, shards, smallest, largest):
    level = 1.0
    for axis_at, shards_of in shards:
        draws = jax.random.uniform(jax.random.fold_in(jax.random.fold_in(rng, 6), axis_at), (shards_of,), jnp.float32, smallest / len(shards), largest / len(shards))
        level = level * jnp.repeat(jnp.exp(draws), dims[axis_at] // shards_of).reshape((-1,) + (1,) * (len(dims) - 1 - axis_at))
    return level


def bell_draw(own_key, shape, deviation, reach, shards=(), kind=jnp.bfloat16):
    result = jax.random.normal(own_key, shape, jnp.float32) * deviation
    if len(shards) > 0:
        result = block_scale(own_key, shape, shards, -0.22, 0.18) * result
    return jnp.clip(result, min=-reach, max=reach).astype(kind)


def setup_inputs(seed: int = 0, part: int = 0) -> dict:
    seeds = jax.random.split(jax.random.key(seed), 16)
    part_keys = jax.random.split(jax.random.fold_in(seeds[15], part), 16)
    return {
        "perturbation": draw_perturbation(jax.random.fold_in(jax.random.fold_in(seeds[15], part), 71), part),
        "base_state": bell_draw(seeds[1], (LEV, NY, 4, NLON), 1.0, 6.0, ((1, 16),), jnp.float32),
        "target_state": bell_draw(seeds[2], (LEV, NY, 4, NLON), 1.0, 6.0, ((1, 16),), jnp.float32),
        "cost_weight": draw_cost_weight(jax.random.fold_in(seeds[15], 71), part),
        "diffusivity": jnp.clip(jnp.exp(math.log(0.2) - 1.609438 * jax.random.uniform(seeds[4], (NY, NLON), jnp.float32) ** block_scale(seeds[4], (NY, NLON), ((0, 16),), -0.2, 0.2)), 0.04, 0.2),
        "chan_mix": bell_draw(seeds[5], (LEV, 4, 4), 4 ** -0.5, 3.0, (), jnp.float32),
        "coupler_mix": bell_draw(seeds[6], (4, 4), 4 ** -0.5, 3.0, (), jnp.float32),
        "owner_mix": bell_draw(seeds[7], (N_HORIZ, N_HORIZ * CAP, N_HORIZ * CAP), (N_HORIZ * CAP) ** -0.5, 0.625, ((0, 16),), jnp.float32),
        "air_temp": bell_draw(seeds[8], (STEPS, N_HORIZ, N_HORIZ * CAP, TILE), 1.0, 6.0, ((1, 16),), jnp.float32),
        "wind_speed": jnp.clip(jnp.exp(math.log(12.0) - 1.7917595 * jax.random.uniform(seeds[9], (STEPS, N_HORIZ, N_HORIZ * CAP, TILE), jnp.float32) ** block_scale(seeds[9], (STEPS, N_HORIZ, N_HORIZ * CAP, TILE), ((1, 16),), -0.2, 0.2)), 2.0, 12.0),
        "wet_list": draw_wet_list(jax.random.fold_in(seeds[15], 71), part),
        "wet_owner": draw_wet_owner(jax.random.fold_in(seeds[15], 71), part),
        "remap_src": draw_remap_src(jax.random.fold_in(seeds[15], 71), part),
        "remap_tgt": draw_remap_tgt(jax.random.fold_in(seeds[15], 71), part),
        "remap_weight": jnp.clip(0.2 + 0.6 * jax.random.uniform(seeds[14], (NREMAP,), jnp.float32) ** block_scale(seeds[14], (NREMAP,), ((0, 16),), -0.2, 0.2), 0.2, 0.8),
    }


KAPPA_V = 0.1
TIME_STEP = 0.3
FLUX_RATE = 0.05
FEEDBACK = 0.5
ASCENT = 0.5
EPSILON = 1e-06

def channel_drive(ocean_field, chan_mix):
    return jnp.tanh(jnp.einsum('lck,ljkx->ljcx', chan_mix, ocean_field, precision=lax.Precision.HIGHEST))

def level_diff(ocean_field):
    padded = jnp.pad(ocean_field, ((1, 1), (0, 0), (0, 0), (0, 0)))
    return padded[2:] + padded[:-2] - 2.0 * ocean_field

def ocean_step(ocean_field, diffusivity, chan_mix):
    padded = jnp.pad(ocean_field, ((0, 0), (1, 1), (0, 0), (0, 0)))
    laplacian = padded[:, 2:] + padded[:, :-2] + jnp.roll(ocean_field, -1, axis=3) + jnp.roll(ocean_field, 1, axis=3) - 4.0 * ocean_field
    return ocean_field + diffusivity[None, :, None, :] * laplacian + KAPPA_V * level_diff(ocean_field) + TIME_STEP * channel_drive(ocean_field, chan_mix)

def bulk_flux(ocean_tiles, mixed, air_field, wind_field, coupler_mix):
    contrast = jnp.concatenate([(air_field - ocean_tiles[..., 0, :])[..., None, :], ocean_tiles[..., 1:, :]], axis=-2)
    contrast = contrast + mixed
    forcing = jnp.einsum('ck,...kx->...cx', coupler_mix, contrast, precision=lax.Precision.HIGHEST)
    return FLUX_RATE * wind_field[..., None, :] * jnp.tanh(forcing)

def reference(perturbation, base_state, target_state, cost_weight, diffusivity, chan_mix, coupler_mix, owner_mix, air_temp, wind_speed, wet_list, wet_owner, remap_src, remap_tgt, remap_weight):
    live_mask = wet_owner >= 0
    onehot = (wet_owner[:, :, None] == jnp.arange(N_HORIZ, dtype=jnp.int32)[None, None, :]).astype(jnp.int32)
    earlier = jnp.cumsum(onehot, axis=1) - onehot
    slot_rank = lax.optimization_barrier(jnp.sum(earlier * onehot, axis=2)).astype(jnp.int32)
    tile_safe = jnp.where(live_mask, wet_list, 0).astype(jnp.int32)
    owner_safe = jnp.where(live_mask, wet_owner, 0).astype(jnp.int32)
    slot_index = (jnp.arange(N_HORIZ, dtype=jnp.int32)[:, None] * CAP + jnp.where(live_mask, slot_rank, 0)).astype(jnp.int32)
    device_index = jnp.broadcast_to(jnp.arange(N_HORIZ, dtype=jnp.int32)[:, None], wet_list.shape)
    live_float = live_mask.astype(jnp.float32)

    def couple(ocean_field, hour_index):
        surface = ocean_field[0]
        tile_view = surface.reshape(N_HORIZ, ROWS_DEV, 4, TPR, TILE).transpose(0, 1, 3, 2, 4)
        tile_view = tile_view.reshape(N_HORIZ, TILES_DEV, 4, TILE)
        picked = tile_view[device_index, tile_safe] * live_float[:, :, None, None]
        received = jnp.zeros((N_HORIZ, N_HORIZ * CAP, 4, TILE), jnp.float32).at[owner_safe, slot_index].add(picked)
        mixed_all = jnp.tanh(jnp.einsum('opq,oqcx->opcx', owner_mix, received, precision=lax.Precision.HIGHEST))
        mixed_here = mixed_all[owner_safe, slot_index]
        air_here = air_temp[hour_index][owner_safe, slot_index]
        wind_here = wind_speed[hour_index][owner_safe, slot_index]
        flux_tiles = bulk_flux(picked, mixed_here, air_here, wind_here, coupler_mix) * live_float[:, :, None, None]
        added = jnp.zeros_like(tile_view).at[device_index, tile_safe].add(flux_tiles)
        surface_add = added.reshape(N_HORIZ, ROWS_DEV, TPR, 4, TILE).transpose(0, 1, 3, 2, 4).reshape(NY, 4, NLON)
        return ocean_field.at[0].add(surface_add)

    def remap(ocean_field):
        surface = ocean_field[0, :, 0, :]
        weighted = surface[remap_src] * remap_weight[:, None]
        summed = jnp.zeros((NLAT, NLON), jnp.float32).at[remap_tgt].add(weighted)
        atmos = jnp.tanh(summed)
        returned = jnp.zeros((NY, NLON), jnp.float32).at[remap_src].add(atmos[remap_tgt] * remap_weight[:, None])
        return ocean_field.at[0, :, 0, :].add(FEEDBACK * returned)

    def forward(start_pert):
        ocean_field = base_state + start_pert
        for hour_index in range(STEPS):
            ocean_field = ocean_step(ocean_field, diffusivity, chan_mix)
            ocean_field = couple(ocean_field, hour_index)
            ocean_field = remap(ocean_field)
        return ocean_field
    final_field, pullback = jax.vjp(forward, perturbation)
    weight_sq = (cost_weight * cost_weight)[None, :, None, :]
    gradient = pullback(weight_sq * (final_field - target_state))[0]
    cell_total = perturbation.size
    mean_pp = jnp.sum(perturbation * perturbation) / cell_total
    mean_pg = jnp.sum(perturbation * gradient) / cell_total
    mean_gg = jnp.sum(gradient * gradient) / cell_total
    grad_scale = lax.rsqrt(mean_gg + EPSILON)
    mean_sq = mean_pp + 2.0 * ASCENT * grad_scale * mean_pg + ASCENT * ASCENT * grad_scale * grad_scale * mean_gg
    stepped = perturbation + ASCENT * grad_scale * gradient
    return stepped * lax.rsqrt(mean_sq + EPSILON)
```

```python
import functools

import jax
import jax.numpy as jnp
from jax import lax
from jax.experimental import pallas as pl
from jax.experimental.pallas import tpu as pltpu
from jax.sharding import PartitionSpec as P

LAT_DEV = 2
PAD = 8

KAPPA_V = 0.1
TIME_STEP = 0.3
FLUX_RATE = 0.05
FEEDBACK = 0.5
ASCENT = 0.5
EPSILON = 1e-06
HIGHEST = lax.Precision.HIGHEST
VMEM_BYTES = 48 * 1024 * 1024


def dot(a, b):
    return jnp.dot(a, b, precision=HIGHEST, preferred_element_type=jnp.float32)


def peer(me, offset, count):
    return lax.rem(me + offset + count, count)


def greet(count):
    me = lax.axis_index("horiz")
    barrier = pltpu.get_barrier_semaphore()

    def signal(offset, carry):
        pl.semaphore_signal(
            barrier, inc=1, device_id={"horiz": peer(me, offset, count)},
            device_id_type=pl.DeviceIdType.MESH,
        )
        return carry

    lax.fori_loop(1, count, signal, 0)
    pl.semaphore_wait(barrier, count - 1)


def block_copy(count, source, target, send, recv, offset):
    me = lax.axis_index("horiz")
    to = peer(me, offset, count)
    return pltpu.make_async_remote_copy(
        src_ref=source.at[to],
        dst_ref=target.at[me],
        send_sem=send.at[offset],
        recv_sem=recv.at[offset],
        device_id={"horiz": to},
        device_id_type=pl.DeviceIdType.MESH,
    )


def exchange(count, source, target, send, recv):
    me = lax.axis_index("horiz")

    def start(offset, carry):
        block_copy(count, source, target, send, recv, offset).start()
        return carry

    def finish(offset, carry):
        block_copy(count, source, target, send, recv, offset).wait()
        return carry

    lax.fori_loop(1, count, start, 0)
    target[me] = source[me]
    lax.fori_loop(1, count, finish, 0)


def shift_copy(count, source, target, sems, at, step):
    me = lax.axis_index("horiz")
    return pltpu.make_async_remote_copy(
        src_ref=source,
        dst_ref=target,
        send_sem=sems.at[at],
        recv_sem=sems.at[at + 1],
        device_id={"horiz": peer(me, step, count)},
        device_id_type=pl.DeviceIdType.MESH,
    )


def remap_sums(count, tiles, mat, sums, got_low, got_high, sems, at):
    me = lax.axis_index("horiz")
    half = sums.shape[0] // 2
    sums[...] = dot(mat[...], tiles[:, 0:128])
    down = shift_copy(count, sums.at[pl.ds(0, half)], got_high, sems, at, -1)
    up = shift_copy(count, sums.at[pl.ds(half, half)], got_low, sems, at + 2, 1)
    down.start()
    up.start()
    down.wait()
    up.wait()
    low = jnp.where(me > 0, got_low[...], 0.0)
    high = jnp.where(me < count - 1, got_high[...], 0.0)
    return jnp.concatenate([sums[0:half] + low, sums[half:] + high], axis=0)


def forward_kernel(
    count, halo, tiles_in, edge_low, edge_high, select, select_t, mat, mat_t, mix, air, wind,
    coupler, tiles, atmos, mixed_out, force_out, halo_low, halo_high, tile_low, tile_high,
    out_buf, in_buf, res_buf, back_buf, sums, got_low, got_high,
    send1, recv1, send2, recv2, sems,
):
    greet(count)
    if halo:
        rest_down = shift_copy(count, edge_low, halo_high, sems, 4, -1)
        rest_up = shift_copy(count, edge_high, halo_low, sems, 6, 1)
        rest_down.start()
        rest_up.start()
    out_buf[...] = dot(select[...], tiles_in[...]).reshape(out_buf.shape)
    exchange(count, out_buf, in_buf, send1, recv1)
    got = in_buf[...].reshape(mixed_out.shape)
    mixed = jnp.tanh(dot(mix[...], got))
    mixed_out[...] = mixed
    contrast = []
    for k in range(4):
        part = got[:, k * 128 : (k + 1) * 128]
        part = air[...] - part if k == 0 else part
        contrast.append(part + mixed[:, k * 128 : (k + 1) * 128])
    for c in range(4):
        force = jnp.tanh(sum(coupler[c, k] * contrast[k] for k in range(4)))
        force_out[:, c * 128 : (c + 1) * 128] = force
        flux = FLUX_RATE * wind[...] * force
        res_buf[:, :, c * 128 : (c + 1) * 128] = flux.reshape(res_buf.shape[:2] + (128,))
    exchange(count, res_buf, back_buf, send2, recv2)
    tiles[...] = tiles_in[...] + dot(select_t[...], back_buf[...].reshape(mixed_out.shape))
    total = jnp.tanh(remap_sums(count, tiles, mat, sums, got_low, got_high, sems, 0))
    atmos[...] = total
    tiles[:, 0:128] = tiles[:, 0:128] + FEEDBACK * dot(mat_t[...], total)
    if halo:
        finish_halo(count, tiles, tile_low, tile_high, sems)
        rest_down.wait()
        rest_up.wait()


def finish_halo(count, tiles, tile_low, tile_high, sems):
    head, tail = tile_high.shape[0], tile_low.shape[0]
    rows = tiles.shape[0]
    down = shift_copy(count, tiles.at[pl.ds(0, head)], tile_high, sems, 8, -1)
    up = shift_copy(count, tiles.at[pl.ds(rows - tail, tail)], tile_low, sems, 10, 1)
    down.start()
    up.start()
    down.wait()
    up.wait()


def adjoint_kernel(
    count, tiles_in, edge_low, edge_high, select, select_t, mat, mat_t, mix_t, wind,
    coupler, atmos, mixed, force, tiles, halo_low, halo_high, tile_low, tile_high,
    out_buf, in_buf, res_buf, back_buf, sums, got_low, got_high,
    send1, recv1, send2, recv2, sems,
):
    greet(count)
    rest_down = shift_copy(count, edge_low, halo_high, sems, 4, -1)
    rest_up = shift_copy(count, edge_high, halo_low, sems, 6, 1)
    tiles[...] = tiles_in[...]
    total = FEEDBACK * remap_sums(count, tiles, mat, sums, got_low, got_high, sems, 0)
    rest_down.start()
    rest_up.start()
    total = total * (1.0 - atmos[...] * atmos[...])
    tiles[:, 0:128] = tiles[:, 0:128] + dot(mat_t[...], total)
    out_buf[...] = dot(select[...], tiles[...]).reshape(out_buf.shape)
    exchange(count, out_buf, in_buf, send1, recv1)
    got = in_buf[...].reshape(mixed.shape)
    dforce = []
    for c in range(4):
        t = force[:, c * 128 : (c + 1) * 128]
        dforce.append(FLUX_RATE * wind[...] * (1.0 - t * t) * got[:, c * 128 : (c + 1) * 128])
    dcontrast = [sum(coupler[c, k] * dforce[c] for c in range(4)) for k in range(4)]
    joined = jnp.concatenate(dcontrast, axis=1)
    signed = jnp.concatenate([-dcontrast[0]] + dcontrast[1:], axis=1)
    held = mixed[...]
    result = signed + dot(mix_t[...], (1.0 - held * held) * joined)
    res_buf[...] = result.reshape(res_buf.shape)
    exchange(count, res_buf, back_buf, send2, recv2)
    tiles[...] = tiles[...] + dot(select_t[...], back_buf[...].reshape(mixed.shape))
    finish_halo(count, tiles, tile_low, tile_high, sems)
    rest_down.wait()
    rest_up.wait()


def sums_kernel(count, mine, total, own, got, send, recv):
    greet(count)
    me = lax.axis_index("horiz")

    def copy(offset):
        return pltpu.make_async_remote_copy(
            src_ref=mine,
            dst_ref=got.at[me],
            send_sem=send.at[offset],
            recv_sem=recv.at[offset],
            device_id={"horiz": peer(me, offset, count)},
            device_id_type=pl.DeviceIdType.MESH,
        )

    def start(offset, carry):
        copy(offset).start()
        return carry

    def finish(offset, carry):
        copy(offset).wait()
        return carry

    lax.fori_loop(1, count, start, 0)
    got[me] = mine[...]
    lax.fori_loop(1, count, finish, 0)
    total[...] = jnp.sum(got[...], axis=0)


def comm_call(kernel, outs, scratch, collective_id, smem_at=None, operands=()):
    specs = [
        pl.BlockSpec(memory_space=pltpu.SMEM if i == smem_at else pltpu.VMEM)
        for i in range(len(operands))
    ]
    return pl.pallas_call(
        kernel,
        out_shape=[jax.ShapeDtypeStruct(s, jnp.float32) for s in outs],
        in_specs=specs,
        out_specs=[pl.BlockSpec(memory_space=pltpu.VMEM)] * len(outs),
        scratch_shapes=scratch,
        compiler_params=pltpu.CompilerParams(
            collective_id=collective_id, has_side_effects=True, vmem_limit_bytes=VMEM_BYTES
        ),
    )(*operands)


def with_halo_permute(block):
    count = lax.axis_size("horiz")
    forward = [(i, i + 1) for i in range(count - 1)]
    backward = [(b, a) for a, b in forward]
    low = lax.ppermute(block[:, -1], "horiz", forward)
    high = lax.ppermute(block[:, 0], "horiz", backward)
    return low, high


def channel_mix_sum(mix, field):
    return jnp.einsum("lck,ljkx->ljcx", mix, field, precision=HIGHEST)


def level_diff(field):
    padded = jnp.pad(field, ((1, 1), (0, 0), (0, 0), (0, 0)))
    return padded[2:] + padded[:-2] - 2.0 * field


def horiz_lap(field, low, high):
    padded = jnp.concatenate([low[:, None], field, high[:, None]], axis=1)
    return (
        padded[:, 2:]
        + padded[:, :-2]
        + jnp.roll(field, -1, axis=3)
        + jnp.roll(field, 1, axis=3)
        - 4.0 * field
    )


def to_tiles(surface, tile_rows):
    row_count, channels, cells = surface.shape
    per_row = cells // 128
    pieces = surface.reshape(row_count, channels, per_row, 128).transpose(0, 2, 1, 3)
    flat = pieces.reshape(row_count * per_row, channels * 128)
    return jnp.pad(flat, ((0, tile_rows - flat.shape[0]), (0, 0)))


def from_tiles(tiles, row_count):
    per_row = tiles.shape[0] // row_count
    pieces = tiles.reshape(row_count, per_row, 4, 128).transpose(0, 2, 1, 3)
    return pieces.reshape(row_count, 4, per_row * 128)


def pad_slots(block, count, capacity, axis):
    shape = block.shape
    split = shape[:axis] + (count, capacity) + shape[axis + 1 :]
    widths = [(0, 0)] * len(split)
    widths[axis + 1] = (0, PAD - capacity)
    padded = jnp.pad(block.reshape(split), widths)
    return padded.reshape(shape[:axis] + (count * PAD,) + shape[axis + 1 :])


def body(
    perturbation,
    base_state,
    target_state,
    cost_weight,
    diffusivity,
    chan_mix,
    coupler_mix,
    owner_mix,
    air_temp,
    wind_speed,
    wet_list,
    wet_owner,
    remap_src,
    remap_tgt,
    remap_weight,
):
    count = lax.axis_size("horiz")
    me = lax.axis_index("horiz")
    levels, row_count, _, cells = base_state.shape
    capacity = air_temp.shape[2] // count
    tile_total = wet_list.shape[1]
    hour_count = air_temp.shape[0]
    per_row = cells // 128
    tile_rows = -(-tile_total // 8) * 8
    slots = count * PAD
    lat_pad = -(-per_row // 8) * 8
    lat_rows = (LAT_DEV + 2) * lat_pad

    owner = wet_owner[0]
    entry = jnp.arange(tile_total, dtype=jnp.int32)
    same = (owner[:, None] == owner[None, :]) & (entry[None, :] < entry[:, None])
    rank = jnp.sum(same.astype(jnp.int32), axis=1)
    slot = jnp.where(owner >= 0, owner * PAD + rank, -1)
    to_slot = (slot[None, :] == jnp.arange(slots, dtype=jnp.int32)[:, None]).astype(jnp.float32)
    of_tile = (wet_list[0][:, None] == jnp.arange(tile_rows, dtype=jnp.int32)[None, :]).astype(
        jnp.float32
    )
    select = dot(to_slot, of_tile)
    select_t = select.T

    src = remap_src - me * row_count
    tgt = remap_tgt - (me * LAT_DEV - 1)
    hit_src = (src[:, None] == jnp.arange(row_count, dtype=jnp.int32)[None, :]).astype(jnp.float32)
    hit_tgt = (tgt[:, None] == jnp.arange(LAT_DEV + 2, dtype=jnp.int32)[None, :]).astype(
        jnp.float32
    )
    small = jnp.sum(
        hit_tgt[:, :, None] * hit_src[:, None, :] * remap_weight[:, None, None], axis=0
    )
    eye = (
        jnp.arange(lat_pad, dtype=jnp.int32)[:, None]
        == jnp.arange(per_row, dtype=jnp.int32)[None, :]
    ).astype(jnp.float32)
    mat = (small[:, None, :, None] * eye[None, :, None, :]).reshape(lat_rows, row_count * per_row)
    mat = jnp.pad(mat, ((0, 0), (0, tile_rows - row_count * per_row)))
    mat_t = mat.T

    mix = pad_slots(pad_slots(owner_mix[0], count, capacity, 0), count, capacity, 1)
    mix_t = mix.T
    air = pad_slots(air_temp[:, 0], count, capacity, 1)
    wind = pad_slots(wind_speed[:, 0], count, capacity, 1)

    head = lat_pad
    tail = tile_rows - (row_count - 1) * per_row // 8 * 8
    tail_skip = (row_count - 1) * per_row - (tile_rows - tail)
    tile_shape = (tile_rows, 512)
    slot_shape = (slots, 512)
    lat_shape = (lat_rows, 128)
    edge_shape = (levels * 4, cells)
    halo_shapes = [edge_shape, edge_shape, (tail, 512), (head, 512)]
    scratch = (
        [pltpu.VMEM((count, PAD, 512), jnp.float32)] * 4
        + [pltpu.VMEM(lat_shape, jnp.float32)]
        + [pltpu.VMEM((lat_rows // 2, 128), jnp.float32)] * 2
        + [pltpu.SemaphoreType.DMA((count,))] * 4
        + [pltpu.SemaphoreType.DMA((12,))]
    )

    def edges(field):
        return field[:, 0].reshape(edge_shape), field[:, -1].reshape(edge_shape)

    def full_halo(low_rest, high_rest, low_tile, high_tile):
        low_top = from_tiles(low_tile[tail_skip : tail_skip + per_row], 1)[0]
        high_top = from_tiles(high_tile[:per_row], 1)[0]
        low = jnp.concatenate([low_top[None], low_rest.reshape(levels, 4, cells)[1:]], axis=0)
        high = jnp.concatenate([high_top[None], high_rest.reshape(levels, 4, cells)[1:]], axis=0)
        return jnp.where(me > 0, low, 0.0), jnp.where(me < count - 1, high, 0.0)

    def with_surface(field, tiles):
        top = from_tiles(tiles[:tile_total], row_count)
        return jnp.concatenate([top[None], field[1:]], axis=0)

    coeff = diffusivity[None, :, None, :]
    field = base_state + perturbation
    extra = jnp.broadcast_to(diffusivity[None, :, None, :], (1, row_count, 4, cells))
    low_all, high_all = with_halo_permute(jnp.concatenate([field, extra], axis=0))
    low, high = low_all[:levels], high_all[:levels]
    coeff_low, coeff_high = low_all[levels:], high_all[levels:]
    saved = []
    for hour in range(hour_count):
        drive = jnp.tanh(channel_mix_sum(chan_mix, field))
        field = (
            field
            + coeff * horiz_lap(field, low, high)
            + KAPPA_V * level_diff(field)
            + TIME_STEP * drive
        )
        edge_low, edge_high = edges(field)
        more = hour + 1 < hour_count
        outs = [tile_shape, lat_shape, slot_shape, slot_shape] + halo_shapes
        tiles, atmos, mixed, force, low_rest, high_rest, low_tile, high_tile = comm_call(
            functools.partial(forward_kernel, count, more),
            outs,
            scratch,
            0 if more else 1,
            smem_at=10,
            operands=(
                to_tiles(field[0], tile_rows), edge_low, edge_high, select, select_t, mat, mat_t,
                mix, air[hour], wind[hour], coupler_mix,
            ),
        )
        field = with_surface(field, tiles)
        if more:
            low, high = full_halo(low_rest, high_rest, low_tile, high_tile)
        saved.append((drive, atmos, mixed, force))
    adjoint = (cost_weight * cost_weight)[None, :, None, :] * (field - target_state)
    for hour in reversed(range(hour_count)):
        drive, atmos, mixed, force = saved[hour]
        edge_low, edge_high = edges(adjoint)
        tiles, low_rest, high_rest, low_tile, high_tile = comm_call(
            functools.partial(adjoint_kernel, count),
            [tile_shape] + halo_shapes,
            scratch,
            2,
            smem_at=9,
            operands=(
                to_tiles(adjoint[0], tile_rows), edge_low, edge_high, select, select_t, mat, mat_t,
                mix_t, wind[hour], coupler_mix, atmos, mixed, force,
            ),
        )
        adjoint = with_surface(adjoint, tiles)
        low, high = full_halo(low_rest, high_rest, low_tile, high_tile)
        adjoint = (
            adjoint
            + horiz_lap(coeff * adjoint, coeff_low * low, coeff_high * high)
            + KAPPA_V * level_diff(adjoint)
            + TIME_STEP
            * jnp.einsum(
                "lck,ljcx->ljkx", chan_mix, (1.0 - drive * drive) * adjoint, precision=HIGHEST
            )
        )
    cell_total = adjoint.size * count
    parts = [
        jnp.sum(perturbation * perturbation),
        jnp.sum(perturbation * adjoint),
        jnp.sum(adjoint * adjoint),
    ]
    row = jnp.arange(8, dtype=jnp.int32)[:, None]
    packed = jnp.broadcast_to(
        jnp.where(row == 0, parts[0], jnp.where(row == 1, parts[1], parts[2])), (8, 128)
    )
    (statistics,) = comm_call(
        functools.partial(sums_kernel, count),
        [(8, 128)],
        [
            pltpu.VMEM((8, 128), jnp.float32),
            pltpu.VMEM((count, 8, 128), jnp.float32),
            pltpu.SemaphoreType.DMA((count,)),
            pltpu.SemaphoreType.DMA((count,)),
        ],
        3,
        operands=(packed,),
    )
    mean_pp = statistics[0, 0] / cell_total
    mean_pg = statistics[1, 0] / cell_total
    mean_gg = statistics[2, 0] / cell_total
    grad_scale = lax.rsqrt(mean_gg + EPSILON)
    mean_sq = (
        mean_pp
        + 2.0 * ASCENT * grad_scale * mean_pg
        + ASCENT * ASCENT * grad_scale * grad_scale * mean_gg
    )
    stepped = perturbation + ASCENT * grad_scale * adjoint
    return stepped * lax.rsqrt(mean_sq + EPSILON)


def solution(mesh):
    placed = (
        P("member", "horiz", None, None),
        P(None, "horiz", None, None),
        P(None, "horiz", None, None),
        P("horiz", None),
        P("horiz", None),
        P(),
        P(),
        P("horiz", None, None),
        P(None, "horiz", None, None),
        P(None, "horiz", None, None),
        P("horiz", None),
        P("horiz", None),
        P("horiz"),
        P("horiz"),
        P("horiz"),
    )
    return jax.shard_map(
        body,
        mesh=mesh,
        in_specs=placed,
        out_specs=P("member", "horiz", None, None),
        check_vma=False,
    )
```

```python
import functools

import jax
import jax.numpy as jnp
from jax import lax
from jax.experimental import pallas as pl
from jax.experimental.pallas import tpu as pltpu
from jax.sharding import PartitionSpec as P

LAT_DEV = 2
PAD = 8

KAPPA_V = 0.1
TIME_STEP = 0.3
FLUX_RATE = 0.05
FEEDBACK = 0.5
ASCENT = 0.5
EPSILON = 1e-06
HIGHEST = lax.Precision.HIGHEST
VMEM_BYTES = 48 * 1024 * 1024


def dot(a, b):
    return jnp.dot(a, b, precision=HIGHEST, preferred_element_type=jnp.float32)


def peer(me, offset, count):
    return lax.rem(me + offset + count, count)


def greet(count):
    me = lax.axis_index("horiz")
    barrier = pltpu.get_barrier_semaphore()

    def signal(offset, carry):
        pl.semaphore_signal(
            barrier, inc=1, device_id={"horiz": peer(me, offset, count)},
            device_id_type=pl.DeviceIdType.MESH,
        )
        return carry

    lax.fori_loop(1, count, signal, 0)
    pl.semaphore_wait(barrier, count - 1)


def block_copy(count, source, target, send, recv, offset):
    me = lax.axis_index("horiz")
    to = peer(me, offset, count)
    return pltpu.make_async_remote_copy(
        src_ref=source.at[to],
        dst_ref=target.at[me],
        send_sem=send.at[offset],
        recv_sem=recv.at[offset],
        device_id={"horiz": to},
        device_id_type=pl.DeviceIdType.MESH,
    )


def exchange(count, source, target, send, recv):
    me = lax.axis_index("horiz")

    def start(offset, carry):
        block_copy(count, source, target, send, recv, offset).start()
        return carry

    def finish(offset, carry):
        block_copy(count, source, target, send, recv, offset).wait()
        return carry

    lax.fori_loop(1, count, start, 0)
    target[me] = source[me]
    lax.fori_loop(1, count, finish, 0)


def shift_copy(count, source, target, sems, at, step):
    me = lax.axis_index("horiz")
    return pltpu.make_async_remote_copy(
        src_ref=source,
        dst_ref=target,
        send_sem=sems.at[at],
        recv_sem=sems.at[at + 1],
        device_id={"horiz": peer(me, step, count)},
        device_id_type=pl.DeviceIdType.MESH,
    )


def neighbours(field, low, high, width, group):
    rows = field.shape[0]
    tile = lax.rem(lax.broadcasted_iota(jnp.int32, field.shape, 0), group)
    lane = lax.broadcasted_iota(jnp.int32, field.shape, 1)
    east = pltpu.roll(field, 127, 1)
    following = jnp.where(
        tile == width - 1, pltpu.roll(east, width - 1, 0), pltpu.roll(east, rows - 1, 0)
    )
    east = jnp.where(lane == 127, following, east)
    west = pltpu.roll(field, 1, 1)
    before = jnp.where(tile == 0, pltpu.roll(west, rows - width + 1, 0), pltpu.roll(west, 1, 0))
    west = jnp.where(lane == 0, before, west)
    north = jnp.concatenate([low, field[: rows - group]], axis=0)
    south = jnp.concatenate([field[group:], high], axis=0)
    return north + south + east + west


def whole_kernel(
    count, width, group, hours, cell_total,
    pert, base, target, cost, coef, select, select_t, mat, mat_t, mix, mix_t, air, wind, chan,
    coupler, out,
    field_a, field_b, drive, halo_low, halo_high, coef_low, coef_high, out_buf, in_buf, mixed_s,
    force_s, atmos_s, sums, got_low, got_high, stat_src, stat_got,
    send, recv, near, stat_send, stat_recv,
):
    me = lax.axis_index("horiz")
    levels, _, rows, _ = pert.shape
    slots = mix.shape[0]
    half = sums.shape[0] // 2
    slot_shape = (slots, 512)
    used = [0, 0, 0]

    def near_copy(source, target_ref, step):
        at = used[0]
        used[0] += 2
        return shift_copy(count, source, target_ref, near, at, step)

    def pair(down_src, down_dst, up_src, up_dst):
        copies = [near_copy(down_src, down_dst, -1), near_copy(up_src, up_dst, 1)]
        for copy in copies:
            copy.start()
        return copies

    def finish(copies):
        for copy in copies:
            copy.wait()

    def halo(ref, at, first, number):
        here = pl.ds(first + 1, number)
        there = pl.ds(first, number)
        return pair(
            ref.at[here, :, pl.ds(0, group)],
            halo_high.at[at, there],
            ref.at[here, :, pl.ds(rows - group, group)],
            halo_low.at[at, there],
        )

    def swap(values):
        at = used[1]
        used[1] += 1
        out_buf[...] = values.reshape(out_buf.shape)
        exchange(count, out_buf, in_buf.at[at], send.at[at], recv.at[at])
        return in_buf[at].reshape(slot_shape)

    def surface(ref):
        return jnp.concatenate([ref[1, c] for c in range(4)], axis=1)

    def add_surface(ref, added):
        for c in range(4):
            ref[1, c] = ref[1, c] + added[:, c * 128 : (c + 1) * 128]

    def remap(ref):
        at = used[2]
        used[2] += 1
        sums[...] = dot(mat[...], ref[1, 0])
        finish(
            pair(
                sums.at[pl.ds(0, half)], got_high.at[at], sums.at[pl.ds(half, half)], got_low.at[at]
            )
        )
        low = jnp.where(me > 0, got_low[at], 0.0)
        high = jnp.where(me < count - 1, got_high[at], 0.0)
        return jnp.concatenate([sums[0:half] + low, sums[half:] + high], axis=0)

    def low_of(at, l, c):
        return jnp.where(me > 0, halo_low[at, l, c], 0.0)

    def high_of(at, l, c):
        return jnp.where(me < count - 1, halo_high[at, l, c], 0.0)

    zeros = jnp.zeros((4, rows, 128), jnp.float32)
    for ref in (field_a, field_b):
        ref[0] = zeros
        ref[levels + 1] = zeros

    def begin(l, total):
        mine = pert[l]
        field_a[l + 1] = base[l] + mine
        return total + jnp.sum(mine * mine, axis=0)

    pp = lax.fori_loop(0, levels, begin, jnp.zeros((rows, 128), jnp.float32))
    greet(count)
    waiting = halo(field_a, 0, 0, levels)
    waiting += pair(
        coef.at[pl.ds(0, group)], coef_high, coef.at[pl.ds(rows - group, group)], coef_low
    )

    def advance(hour, old, new):
        def level(l, carry):
            xs = [old[l + 1, c] for c in range(4)]
            for c in range(4):
                pushed = jnp.tanh(sum(chan[l * 16 + c * 4 + k] * xs[k] for k in range(4)))
                drive[hour, l, c] = pushed
                around = neighbours(xs[c], low_of(hour, l, c), high_of(hour, l, c), width, group)
                new[l + 1, c] = (
                    xs[c]
                    + coef[...] * (around - 4.0 * xs[c])
                    + KAPPA_V * (old[l, c] + old[l + 2, c] - 2.0 * xs[c])
                    + TIME_STEP * pushed
                )
            return carry

        lax.fori_loop(0, levels, level, 0)

    old, new = field_a, field_b
    for hour in range(hours):
        finish(waiting)
        advance(hour, old, new)
        more = hour + 1 < hours
        waiting = halo(new, hour + 1, 1, levels - 1) if more else []
        got = swap(dot(select[...], surface(new)))
        mixed = jnp.tanh(dot(mix[...], got))
        mixed_s[hour] = mixed
        contrast = []
        for k in range(4):
            part = got[:, k * 128 : (k + 1) * 128]
            part = air[hour] - part if k == 0 else part
            contrast.append(part + mixed[:, k * 128 : (k + 1) * 128])
        force = [
            jnp.tanh(sum(coupler[c, k] * contrast[k] for k in range(4))) for c in range(4)
        ]
        force_s[hour] = jnp.concatenate(force, axis=1)
        scaled = FLUX_RATE * wind[hour]
        back = swap(jnp.concatenate([scaled * f for f in force], axis=1))
        add_surface(new, dot(select_t[...], back))
        total = jnp.tanh(remap(new))
        atmos_s[hour] = total
        new[1, 0] = new[1, 0] + FEEDBACK * dot(mat_t[...], total)
        if more:
            waiting += halo(new, hour + 1, 0, 1)
        old, new = new, old

    def turn(l, carry):
        for c in range(4):
            new[l + 1, c] = cost[...] * cost[...] * (old[l + 1, c] - target[l, c])
        return carry

    lax.fori_loop(0, levels, turn, 0)
    old, new = new, old

    def retreat(hour, at, old, new, last):
        real = lax.rem(lax.broadcasted_iota(jnp.int32, (rows, 128), 0), group) < width
        factor = coef[...]

        def level(l, carry):
            pg, gg = carry
            adj = [old[l + 1, c] for c in range(4)]
            weighted = []
            for c in range(4):
                pushed = drive[hour, l, c]
                weighted.append((1.0 - pushed * pushed) * adj[c])
            for k in range(4):
                spread = factor * adj[k]
                around = neighbours(
                    spread, coef_low[...] * low_of(at, l, k), coef_high[...] * high_of(at, l, k),
                    width, group,
                )
                result = (
                    adj[k]
                    + jnp.where(real, around - 4.0 * spread, 0.0)
                    + KAPPA_V * (old[l, k] + old[l + 2, k] - 2.0 * adj[k])
                    + TIME_STEP * sum(chan[l * 16 + c * 4 + k] * weighted[c] for c in range(4))
                )
                new[l + 1, k] = result
                if last:
                    pg = pg + pert[l, k] * result
                    gg = gg + result * result
            return pg, gg

        start = jnp.zeros((rows, 128), jnp.float32)
        return lax.fori_loop(0, levels, level, (start, start))

    for hour in reversed(range(hours)):
        at = 2 * hours - 1 - hour
        total = FEEDBACK * remap(old)
        waiting = halo(old, at, 1, levels - 1)
        total = total * (1.0 - atmos_s[hour] * atmos_s[hour])
        old[1, 0] = old[1, 0] + dot(mat_t[...], total)
        got = swap(dot(select[...], surface(old)))
        scaled = FLUX_RATE * wind[hour]
        dforce = []
        for c in range(4):
            t = force_s[hour, :, c * 128 : (c + 1) * 128]
            dforce.append(scaled * (1.0 - t * t) * got[:, c * 128 : (c + 1) * 128])
        dcontrast = [sum(coupler[c, k] * dforce[c] for c in range(4)) for k in range(4)]
        joined = jnp.concatenate(dcontrast, axis=1)
        signed = jnp.concatenate([-dcontrast[0]] + dcontrast[1:], axis=1)
        held = mixed_s[hour]
        back = swap(signed + dot(mix_t[...], (1.0 - held * held) * joined))
        add_surface(old, dot(select_t[...], back))
        waiting += halo(old, at, 0, 1)
        finish(waiting)
        pg, gg = retreat(hour, at, old, new, hour == 0)
        old, new = new, old

    for i, value in enumerate((pp, pg, gg)):
        value = value if value.ndim == 2 else jnp.sum(value, axis=0)
        stat_src[i * 8 : (i + 1) * 8] = jnp.sum(value.reshape(rows // 8, 8, 128), axis=0)

    def stat_copy(offset):
        return pltpu.make_async_remote_copy(
            src_ref=stat_src,
            dst_ref=stat_got.at[me],
            send_sem=stat_send.at[offset],
            recv_sem=stat_recv.at[offset],
            device_id={"horiz": peer(me, offset, count)},
            device_id_type=pl.DeviceIdType.MESH,
        )

    def stat_start(offset, carry):
        stat_copy(offset).start()
        return carry

    def stat_finish(offset, carry):
        stat_copy(offset).wait()
        return carry

    lax.fori_loop(1, count, stat_start, 0)
    stat_got[me] = stat_src[...]
    lax.fori_loop(1, count, stat_finish, 0)
    stats = jnp.sum(stat_got[...], axis=0)
    mean_pp, mean_pg, mean_gg = [
        jnp.sum(stats[i * 8 : (i + 1) * 8], axis=(0, 1), keepdims=True) / cell_total
        for i in range(3)
    ]
    grad_scale = lax.rsqrt(mean_gg + EPSILON)
    mean_sq = (
        mean_pp
        + 2.0 * ASCENT * grad_scale * mean_pg
        + ASCENT * ASCENT * grad_scale * grad_scale * mean_gg
    )
    norm = lax.rsqrt(mean_sq + EPSILON)

    def close(l, carry):
        for c in range(4):
            out[l, c] = (pert[l, c] + ASCENT * grad_scale * old[l + 1, c]) * norm
        return carry

    lax.fori_loop(0, levels, close, 0)


def pad_slots(block, count, capacity, axis):
    shape = block.shape
    split = shape[:axis] + (count, capacity) + shape[axis + 1 :]
    widths = [(0, 0)] * len(split)
    widths[axis + 1] = (0, PAD - capacity)
    padded = jnp.pad(block.reshape(split), widths)
    return padded.reshape(shape[:axis] + (count * PAD,) + shape[axis + 1 :])


def body(
    perturbation,
    base_state,
    target_state,
    cost_weight,
    diffusivity,
    chan_mix,
    coupler_mix,
    owner_mix,
    air_temp,
    wind_speed,
    wet_list,
    wet_owner,
    remap_src,
    remap_tgt,
    remap_weight,
):
    count = lax.axis_size("horiz")
    me = lax.axis_index("horiz")
    levels, row_count, _, cells = base_state.shape
    capacity = air_temp.shape[2] // count
    tile_total = wet_list.shape[1]
    hour_count = air_temp.shape[0]
    width = cells // 128
    group = -(-width // 8) * 8
    rows = row_count * group
    slots = count * PAD
    lat_rows = (LAT_DEV + 2) * group

    owner = wet_owner[0]
    entry = jnp.arange(tile_total, dtype=jnp.int32)
    same = (owner[:, None] == owner[None, :]) & (entry[None, :] < entry[:, None])
    rank = jnp.sum(same.astype(jnp.int32), axis=1)
    slot = jnp.where(owner >= 0, owner * PAD + rank, -1)
    to_slot = (slot[None, :] == jnp.arange(slots, dtype=jnp.int32)[:, None]).astype(jnp.float32)
    place = jnp.where(owner >= 0, wet_list[0] // width * group + wet_list[0] % width, -1)
    of_tile = (place[:, None] == jnp.arange(rows, dtype=jnp.int32)[None, :]).astype(jnp.float32)
    select = dot(to_slot, of_tile)

    src = remap_src - me * row_count
    tgt = remap_tgt - (me * LAT_DEV - 1)
    hit_src = (src[:, None] == jnp.arange(row_count, dtype=jnp.int32)[None, :]).astype(jnp.float32)
    hit_tgt = (tgt[:, None] == jnp.arange(LAT_DEV + 2, dtype=jnp.int32)[None, :]).astype(
        jnp.float32
    )
    small = jnp.sum(
        hit_tgt[:, :, None] * hit_src[:, None, :] * remap_weight[:, None, None], axis=0
    )
    index = jnp.arange(group, dtype=jnp.int32)
    eye = (index[:, None] == index[None, :]).astype(jnp.float32)
    mat = (small[:, None, :, None] * eye[None, :, None, :]).reshape(lat_rows, rows)

    mix = pad_slots(pad_slots(owner_mix[0], count, capacity, 0), count, capacity, 1)
    air = pad_slots(air_temp[:, 0], count, capacity, 1)
    wind = pad_slots(wind_speed[:, 0], count, capacity, 1)

    def to_tiles(field):
        pieces = field.reshape(levels, row_count, 4, width, 128).transpose(0, 2, 1, 3, 4)
        widths = ((0, 0), (0, 0), (0, 0), (0, group - width), (0, 0))
        return jnp.pad(pieces, widths).reshape(levels, 4, rows, 128)

    def column_tiles(column):
        pieces = column.reshape(row_count, width, 128)
        return jnp.pad(pieces, ((0, 0), (0, group - width), (0, 0))).reshape(rows, 128)

    f32 = jnp.float32
    rounds = 2 * hour_count
    operands = (
        to_tiles(perturbation), to_tiles(base_state), to_tiles(target_state),
        column_tiles(cost_weight), column_tiles(diffusivity), select, select.T, mat, mat.T, mix,
        mix.T, air, wind, chan_mix.reshape(-1), coupler_mix,
    )
    specs = [pl.BlockSpec(memory_space=pltpu.VMEM)] * (len(operands) - 2)
    specs += [pl.BlockSpec(memory_space=pltpu.SMEM)] * 2
    result = pl.pallas_call(
        functools.partial(
            whole_kernel, count, width, group, hour_count, perturbation.size * count
        ),
        out_shape=jax.ShapeDtypeStruct((levels, 4, rows, 128), f32),
        in_specs=specs,
        out_specs=pl.BlockSpec(memory_space=pltpu.VMEM),
        scratch_shapes=[
            pltpu.VMEM((levels + 2, 4, rows, 128), f32),
            pltpu.VMEM((levels + 2, 4, rows, 128), f32),
            pltpu.VMEM((hour_count, levels, 4, rows, 128), f32),
            pltpu.VMEM((rounds, levels, 4, group, 128), f32),
            pltpu.VMEM((rounds, levels, 4, group, 128), f32),
            pltpu.VMEM((group, 128), f32),
            pltpu.VMEM((group, 128), f32),
            pltpu.VMEM((count, PAD, 512), f32),
            pltpu.VMEM((2 * rounds, count, PAD, 512), f32),
            pltpu.VMEM((hour_count, slots, 512), f32),
            pltpu.VMEM((hour_count, slots, 512), f32),
            pltpu.VMEM((hour_count, lat_rows, 128), f32),
            pltpu.VMEM((lat_rows, 128), f32),
            pltpu.VMEM((rounds, lat_rows // 2, 128), f32),
            pltpu.VMEM((rounds, lat_rows // 2, 128), f32),
            pltpu.VMEM((24, 128), f32),
            pltpu.VMEM((count, 24, 128), f32),
            pltpu.SemaphoreType.DMA((2 * rounds, count)),
            pltpu.SemaphoreType.DMA((2 * rounds, count)),
            pltpu.SemaphoreType.DMA((16 * rounds,)),
            pltpu.SemaphoreType.DMA((count,)),
            pltpu.SemaphoreType.DMA((count,)),
        ],
        compiler_params=pltpu.CompilerParams(
            collective_id=0, has_side_effects=True, vmem_limit_bytes=VMEM_BYTES
        ),
    )(*operands)
    pieces = result.reshape(levels, 4, row_count, group, 128)[:, :, :, :width]
    return pieces.transpose(0, 2, 1, 3, 4).reshape(perturbation.shape)


def solution(mesh):
    placed = (
        P("member", "horiz", None, None),
        P(None, "horiz", None, None),
        P(None, "horiz", None, None),
        P("horiz", None),
        P("horiz", None),
        P(),
        P(),
        P("horiz", None, None),
        P(None, "horiz", None, None),
        P(None, "horiz", None, None),
        P("horiz", None),
        P("horiz", None),
        P("horiz"),
        P("horiz"),
        P("horiz"),
    )
    return jax.shard_map(
        body,
        mesh=mesh,
        in_specs=placed,
        out_specs=P("member", "horiz", None, None),
        check_vma=False,
    )
```

```python
import functools

import jax
import jax.numpy as jnp
from jax import lax
from jax.experimental import pallas as pl
from jax.experimental.pallas import tpu as pltpu
from jax.sharding import PartitionSpec as P

LAT_DEV = 2
PAD = 8

KAPPA_V = 0.1
TIME_STEP = 0.3
FLUX_RATE = 0.05
FEEDBACK = 0.5
ASCENT = 0.5
EPSILON = 1e-06
HIGHEST = lax.Precision.HIGHEST
VMEM_BYTES = 48 * 1024 * 1024


def dot(a, b):
    return jnp.dot(a, b, precision=HIGHEST, preferred_element_type=jnp.float32)


def dot_t(a, b):
    return lax.dot_general(
        a, b, (((0,), (0,)), ((), ())), precision=HIGHEST, preferred_element_type=jnp.float32
    )


def peer(me, offset, count):
    return lax.rem(me + offset + count, count)


def greet(count):
    me = lax.axis_index("horiz")
    barrier = pltpu.get_barrier_semaphore()

    def signal(offset, carry):
        pl.semaphore_signal(
            barrier, inc=1, device_id={"horiz": peer(me, offset, count)},
            device_id_type=pl.DeviceIdType.MESH,
        )
        return carry

    lax.fori_loop(1, count, signal, 0)
    return lambda: pl.semaphore_wait(barrier, count - 1)


def block_copy(count, capacity, source, target, send, recv, offset):
    me = lax.axis_index("horiz")
    to = peer(me, offset, count)
    return pltpu.make_async_remote_copy(
        src_ref=source.at[to, pl.ds(0, capacity)],
        dst_ref=target.at[me, pl.ds(0, capacity)],
        send_sem=send.at[offset],
        recv_sem=recv.at[offset],
        device_id={"horiz": to},
        device_id_type=pl.DeviceIdType.MESH,
    )


def exchange(count, capacity, source, target, send, recv):
    me = lax.axis_index("horiz")

    def start(offset, carry):
        block_copy(count, capacity, source, target, send, recv, offset).start()
        return carry

    def finish(offset, carry):
        block_copy(count, capacity, source, target, send, recv, offset).wait()
        return carry

    lax.fori_loop(1, count, start, 0)
    target[me] = source[me]
    lax.fori_loop(1, count, finish, 0)


def shift_copy(count, source, target, sems, at, step):
    me = lax.axis_index("horiz")
    return pltpu.make_async_remote_copy(
        src_ref=source,
        dst_ref=target,
        send_sem=sems.at[at],
        recv_sem=sems.at[at + 1],
        device_id={"horiz": peer(me, step, count)},
        device_id_type=pl.DeviceIdType.MESH,
    )


def neighbours(field, low, high, width, group):
    rows = field.shape[0]
    tile = lax.rem(lax.broadcasted_iota(jnp.int32, field.shape, 0), group)
    lane = lax.broadcasted_iota(jnp.int32, field.shape, 1)
    east = pltpu.roll(field, 127, 1)
    following = jnp.where(
        tile == width - 1, pltpu.roll(east, width - 1, 0), pltpu.roll(east, rows - 1, 0)
    )
    east = jnp.where(lane == 127, following, east)
    west = pltpu.roll(field, 1, 1)
    before = jnp.where(tile == 0, pltpu.roll(west, rows - width + 1, 0), pltpu.roll(west, 1, 0))
    west = jnp.where(lane == 0, before, west)
    north = jnp.concatenate([low, field[: rows - group]], axis=0)
    south = jnp.concatenate([field[group:], high], axis=0)
    return north + south + east + west


def whole_kernel(
    count, width, group, hours, cell_total,
    pert, base, target, cost, coef, select, mat, mix_in, air_in, wind_in, chan, coupler, out,
    mix, air, wind, field_a, field_b, drive, halo_low, halo_high, coef_low, coef_high, out_buf, in_buf, mixed_s,
    force_s, atmos_s, sums, got_low, got_high, stat_src, stat_got,
    send, recv, near, stat_send, stat_recv,
):
    me = lax.axis_index("horiz")
    levels, _, rows, _ = pert.shape
    slots = mix.shape[0]
    capacity = mix_in.shape[1] // count
    half = sums.shape[0] // 2
    slot_shape = (slots, 512)
    used = [0, 0, 0]

    def near_copy(source, target_ref, step):
        at = used[0]
        used[0] += 2
        return shift_copy(count, source, target_ref, near, at, step)

    def pair(down_src, down_dst, up_src, up_dst):
        copies = [near_copy(down_src, down_dst, -1), near_copy(up_src, up_dst, 1)]
        for copy in copies:
            copy.start()
        return copies

    def finish(copies):
        for copy in copies:
            copy.wait()

    def halo(ref, at, first, number):
        here = pl.ds(first + 1, number)
        there = pl.ds(first, number)
        return pair(
            ref.at[here, :, pl.ds(0, group)],
            halo_high.at[at, there],
            ref.at[here, :, pl.ds(rows - group, group)],
            halo_low.at[at, there],
        )

    def swap(values):
        at = used[1]
        used[1] += 1
        out_buf[...] = values.reshape(out_buf.shape)
        exchange(count, capacity, out_buf, in_buf.at[at], send.at[at], recv.at[at])
        return in_buf[at].reshape(slot_shape)

    def surface(ref):
        return jnp.concatenate([ref[1, c] for c in range(4)], axis=1)

    def add_surface(ref, added):
        for c in range(4):
            ref[1, c] = ref[1, c] + added[:, c * 128 : (c + 1) * 128]

    def remap(ref):
        at = used[2]
        used[2] += 1
        sums[...] = dot(mat[...], ref[1, 0])
        finish(
            pair(
                sums.at[pl.ds(0, half)], got_high.at[at], sums.at[pl.ds(half, half)], got_low.at[at]
            )
        )
        low = jnp.where(me > 0, got_low[at], 0.0)
        high = jnp.where(me < count - 1, got_high[at], 0.0)
        return jnp.concatenate([sums[0:half] + low, sums[half:] + high], axis=0)

    def low_of(at, l, c):
        return jnp.where(me > 0, halo_low[at, l, c], 0.0)

    def high_of(at, l, c):
        return jnp.where(me < count - 1, halo_high[at, l, c], 0.0)

    for at in range(in_buf.shape[0]):
        in_buf[at, :, capacity:] = jnp.zeros((count, PAD - capacity, 512), jnp.float32)
    all_in = greet(count)
    zeros = jnp.zeros((4, rows, 128), jnp.float32)
    for ref in (field_a, field_b):
        ref[0] = zeros
        ref[levels + 1] = zeros

    def begin(l, total):
        mine = pert[l]
        field_a[l + 1] = base[l] + mine
        return total + jnp.sum(mine * mine, axis=0)

    pp = lax.fori_loop(0, levels, begin, jnp.zeros((rows, 128), jnp.float32))
    all_in()
    waiting = halo(field_a, 0, 0, levels)
    waiting += pair(
        coef.at[pl.ds(0, group)], coef_high, coef.at[pl.ds(rows - group, group)], coef_low
    )
    slot = lax.broadcasted_iota(jnp.int32, (slots, count * capacity), 0)
    cell = lax.broadcasted_iota(jnp.int32, (slots, count * capacity), 1)
    rank = slot % PAD
    widen = ((slot // PAD * capacity + rank == cell) & (rank < capacity)).astype(jnp.float32)
    mix[...] = lax.dot_general(
        dot(widen, mix_in[0]), widen, (((1,), (1,)), ((), ())), precision=HIGHEST,
        preferred_element_type=jnp.float32,
    )
    for hour in range(hours):
        air[hour] = dot(widen, air_in[hour, 0])
        wind[hour] = dot(widen, wind_in[hour, 0])

    def advance(hour, old, new):
        def level(l, carry):
            xs = [old[l + 1, c] for c in range(4)]
            for c in range(4):
                pushed = jnp.tanh(sum(chan[l * 16 + c * 4 + k] * xs[k] for k in range(4)))
                drive[hour, l, c] = pushed
                around = neighbours(xs[c], low_of(hour, l, c), high_of(hour, l, c), width, group)
                new[l + 1, c] = (
                    xs[c]
                    + coef[...] * (around - 4.0 * xs[c])
                    + KAPPA_V * (old[l, c] + old[l + 2, c] - 2.0 * xs[c])
                    + TIME_STEP * pushed
                )
            return carry

        lax.fori_loop(0, levels, level, 0)

    old, new = field_a, field_b
    for hour in range(hours):
        finish(waiting)
        advance(hour, old, new)
        more = hour + 1 < hours
        waiting = halo(new, hour + 1, 1, levels - 1) if more else []
        got = swap(dot(select[...], surface(new)))
        mixed = jnp.tanh(dot(mix[...], got))
        mixed_s[hour] = mixed
        contrast = []
        for k in range(4):
            part = got[:, k * 128 : (k + 1) * 128]
            part = air[hour] - part if k == 0 else part
            contrast.append(part + mixed[:, k * 128 : (k + 1) * 128])
        force = [
            jnp.tanh(sum(coupler[c, k] * contrast[k] for k in range(4))) for c in range(4)
        ]
        force_s[hour] = jnp.concatenate(force, axis=1)
        scaled = FLUX_RATE * wind[hour]
        back = swap(jnp.concatenate([scaled * f for f in force], axis=1))
        add_surface(new, dot_t(select[...], back))
        total = jnp.tanh(remap(new))
        atmos_s[hour] = total
        new[1, 0] = new[1, 0] + FEEDBACK * dot_t(mat[...], total)
        if more:
            waiting += halo(new, hour + 1, 0, 1)
        old, new = new, old

    def turn(l, carry):
        for c in range(4):
            new[l + 1, c] = cost[...] * cost[...] * (old[l + 1, c] - target[l, c])
        return carry

    lax.fori_loop(0, levels, turn, 0)
    old, new = new, old

    def retreat(hour, at, old, new, last):
        real = lax.rem(lax.broadcasted_iota(jnp.int32, (rows, 128), 0), group) < width
        factor = coef[...]

        def level(l, carry):
            pg, gg = carry
            adj = [old[l + 1, c] for c in range(4)]
            weighted = []
            for c in range(4):
                pushed = drive[hour, l, c]
                weighted.append((1.0 - pushed * pushed) * adj[c])
            for k in range(4):
                spread = factor * adj[k]
                around = neighbours(
                    spread, coef_low[...] * low_of(at, l, k), coef_high[...] * high_of(at, l, k),
                    width, group,
                )
                result = (
                    adj[k]
                    + jnp.where(real, around - 4.0 * spread, 0.0)
                    + KAPPA_V * (old[l, k] + old[l + 2, k] - 2.0 * adj[k])
                    + TIME_STEP * sum(chan[l * 16 + c * 4 + k] * weighted[c] for c in range(4))
                )
                new[l + 1, k] = result
                if last:
                    pg = pg + pert[l, k] * result
                    gg = gg + result * result
            return pg, gg

        start = jnp.zeros((rows, 128), jnp.float32)
        return lax.fori_loop(0, levels, level, (start, start))

    for hour in reversed(range(hours)):
        at = 2 * hours - 1 - hour
        total = FEEDBACK * remap(old)
        waiting = halo(old, at, 1, levels - 1)
        total = total * (1.0 - atmos_s[hour] * atmos_s[hour])
        old[1, 0] = old[1, 0] + dot_t(mat[...], total)
        got = swap(dot(select[...], surface(old)))
        scaled = FLUX_RATE * wind[hour]
        dforce = []
        for c in range(4):
            t = force_s[hour, :, c * 128 : (c + 1) * 128]
            dforce.append(scaled * (1.0 - t * t) * got[:, c * 128 : (c + 1) * 128])
        dcontrast = [sum(coupler[c, k] * dforce[c] for c in range(4)) for k in range(4)]
        joined = jnp.concatenate(dcontrast, axis=1)
        signed = jnp.concatenate([-dcontrast[0]] + dcontrast[1:], axis=1)
        held = mixed_s[hour]
        back = swap(signed + dot_t(mix[...], (1.0 - held * held) * joined))
        add_surface(old, dot_t(select[...], back))
        waiting += halo(old, at, 0, 1)
        finish(waiting)
        pg, gg = retreat(hour, at, old, new, hour == 0)
        old, new = new, old

    for i, value in enumerate((pp, pg, gg)):
        value = value if value.ndim == 2 else jnp.sum(value, axis=0)
        stat_src[i * 8 : (i + 1) * 8] = jnp.sum(value.reshape(rows // 8, 8, 128), axis=0)

    def stat_copy(offset):
        return pltpu.make_async_remote_copy(
            src_ref=stat_src,
            dst_ref=stat_got.at[me],
            send_sem=stat_send.at[offset],
            recv_sem=stat_recv.at[offset],
            device_id={"horiz": peer(me, offset, count)},
            device_id_type=pl.DeviceIdType.MESH,
        )

    def stat_start(offset, carry):
        stat_copy(offset).start()
        return carry

    def stat_finish(offset, carry):
        stat_copy(offset).wait()
        return carry

    lax.fori_loop(1, count, stat_start, 0)
    stat_got[me] = stat_src[...]
    lax.fori_loop(1, count, stat_finish, 0)
    stats = jnp.sum(stat_got[...], axis=0)
    mean_pp, mean_pg, mean_gg = [
        jnp.sum(stats[i * 8 : (i + 1) * 8], axis=(0, 1), keepdims=True) / cell_total
        for i in range(3)
    ]
    grad_scale = lax.rsqrt(mean_gg + EPSILON)
    mean_sq = (
        mean_pp
        + 2.0 * ASCENT * grad_scale * mean_pg
        + ASCENT * ASCENT * grad_scale * grad_scale * mean_gg
    )
    norm = lax.rsqrt(mean_sq + EPSILON)

    def close(l, carry):
        for c in range(4):
            out[l, c] = (pert[l, c] + ASCENT * grad_scale * old[l + 1, c]) * norm
        return carry

    lax.fori_loop(0, levels, close, 0)


def body(
    perturbation,
    base_state,
    target_state,
    cost_weight,
    diffusivity,
    chan_mix,
    coupler_mix,
    owner_mix,
    air_temp,
    wind_speed,
    wet_list,
    wet_owner,
    remap_src,
    remap_tgt,
    remap_weight,
):
    count = lax.axis_size("horiz")
    me = lax.axis_index("horiz")
    levels, row_count, _, cells = base_state.shape
    tile_total = wet_list.shape[1]
    hour_count = air_temp.shape[0]
    width = cells // 128
    group = -(-width // 8) * 8
    rows = row_count * group
    slots = count * PAD
    lat_rows = (LAT_DEV + 2) * group

    owner = wet_owner[0]
    entry = jnp.arange(tile_total, dtype=jnp.int32)
    same = (owner[:, None] == owner[None, :]) & (entry[None, :] < entry[:, None])
    rank = jnp.sum(same.astype(jnp.int32), axis=1)
    slot = jnp.where(owner >= 0, owner * PAD + rank, -1)
    to_slot = (slot[None, :] == jnp.arange(slots, dtype=jnp.int32)[:, None]).astype(jnp.float32)
    place = jnp.where(owner >= 0, wet_list[0] // width * group + wet_list[0] % width, -1)
    of_tile = (place[:, None] == jnp.arange(rows, dtype=jnp.int32)[None, :]).astype(jnp.float32)
    select = dot(to_slot, of_tile)

    src = remap_src - me * row_count
    tgt = remap_tgt - (me * LAT_DEV - 1)
    hit_src = (src[:, None] == jnp.arange(row_count, dtype=jnp.int32)[None, :]).astype(jnp.float32)
    hit_tgt = (tgt[:, None] == jnp.arange(LAT_DEV + 2, dtype=jnp.int32)[None, :]).astype(
        jnp.float32
    )
    small = jnp.sum(
        hit_tgt[:, :, None] * hit_src[:, None, :] * remap_weight[:, None, None], axis=0
    )
    index = jnp.arange(group, dtype=jnp.int32)
    eye = (index[:, None] == index[None, :]).astype(jnp.float32)
    mat = (small[:, None, :, None] * eye[None, :, None, :]).reshape(lat_rows, rows)

    def to_tiles(field):
        pieces = field.reshape(levels, row_count, 4, width, 128).transpose(0, 2, 1, 3, 4)
        widths = ((0, 0), (0, 0), (0, 0), (0, group - width), (0, 0))
        return jnp.pad(pieces, widths).reshape(levels, 4, rows, 128)

    def column_tiles(column):
        pieces = column.reshape(row_count, width, 128)
        return jnp.pad(pieces, ((0, 0), (0, group - width), (0, 0))).reshape(rows, 128)

    f32 = jnp.float32
    rounds = 2 * hour_count
    operands = (
        to_tiles(perturbation), to_tiles(base_state), to_tiles(target_state),
        column_tiles(cost_weight), column_tiles(diffusivity), select, mat, owner_mix, air_temp,
        wind_speed, chan_mix.reshape(-1), coupler_mix,
    )
    specs = [pl.BlockSpec(memory_space=pltpu.VMEM)] * (len(operands) - 2)
    specs += [pl.BlockSpec(memory_space=pltpu.SMEM)] * 2
    result = pl.pallas_call(
        functools.partial(
            whole_kernel, count, width, group, hour_count, perturbation.size * count
        ),
        out_shape=jax.ShapeDtypeStruct((levels, 4, rows, 128), f32),
        in_specs=specs,
        out_specs=pl.BlockSpec(memory_space=pltpu.VMEM),
        scratch_shapes=[
            pltpu.VMEM((slots, slots), f32),
            pltpu.VMEM((hour_count, slots, 128), f32),
            pltpu.VMEM((hour_count, slots, 128), f32),
            pltpu.VMEM((levels + 2, 4, rows, 128), f32),
            pltpu.VMEM((levels + 2, 4, rows, 128), f32),
            pltpu.VMEM((hour_count, levels, 4, rows, 128), f32),
            pltpu.VMEM((rounds, levels, 4, group, 128), f32),
            pltpu.VMEM((rounds, levels, 4, group, 128), f32),
            pltpu.VMEM((group, 128), f32),
            pltpu.VMEM((group, 128), f32),
            pltpu.VMEM((count, PAD, 512), f32),
            pltpu.VMEM((2 * rounds, count, PAD, 512), f32),
            pltpu.VMEM((hour_count, slots, 512), f32),
            pltpu.VMEM((hour_count, slots, 512), f32),
            pltpu.VMEM((hour_count, lat_rows, 128), f32),
            pltpu.VMEM((lat_rows, 128), f32),
            pltpu.VMEM((rounds, lat_rows // 2, 128), f32),
            pltpu.VMEM((rounds, lat_rows // 2, 128), f32),
            pltpu.VMEM((24, 128), f32),
            pltpu.VMEM((count, 24, 128), f32),
            pltpu.SemaphoreType.DMA((2 * rounds, count)),
            pltpu.SemaphoreType.DMA((2 * rounds, count)),
            pltpu.SemaphoreType.DMA((16 * rounds,)),
            pltpu.SemaphoreType.DMA((count,)),
            pltpu.SemaphoreType.DMA((count,)),
        ],
        compiler_params=pltpu.CompilerParams(
            collective_id=0, has_side_effects=True, vmem_limit_bytes=VMEM_BYTES
        ),
    )(*operands)
    pieces = result.reshape(levels, 4, row_count, group, 128)[:, :, :, :width]
    return pieces.transpose(0, 2, 1, 3, 4).reshape(perturbation.shape)


def solution(mesh):
    placed = (
        P("member", "horiz", None, None),
        P(None, "horiz", None, None),
        P(None, "horiz", None, None),
        P("horiz", None),
        P("horiz", None),
        P(),
        P(),
        P("horiz", None, None),
        P(None, "horiz", None, None),
        P(None, "horiz", None, None),
        P("horiz", None),
        P("horiz", None),
        P("horiz"),
        P("horiz"),
        P("horiz"),
    )
    return jax.shard_map(
        body,
        mesh=mesh,
        in_specs=placed,
        out_specs=P("member", "horiz", None, None),
        check_vma=False,
    )
```

```python
import functools

import jax
import jax.numpy as jnp
from jax import lax
from jax.experimental import pallas as pl
from jax.experimental.pallas import tpu as pltpu
from jax.sharding import PartitionSpec as P

LAT_DEV = 2
PAD = 8

KAPPA_V = 0.1
TIME_STEP = 0.3
FLUX_RATE = 0.05
FEEDBACK = 0.5
ASCENT = 0.5
EPSILON = 1e-06
HIGHEST = lax.Precision.HIGHEST
VMEM_BYTES = 48 * 1024 * 1024


def dot(a, b):
    return jnp.dot(a, b, precision=HIGHEST, preferred_element_type=jnp.float32)


def dot_t(a, b):
    return lax.dot_general(
        a, b, (((0,), (0,)), ((), ())), precision=HIGHEST, preferred_element_type=jnp.float32
    )


def peer(me, offset, count):
    return lax.rem(me + offset + count, count)


def greet(count):
    me = lax.axis_index("horiz")
    barrier = pltpu.get_barrier_semaphore()

    def signal(offset, carry):
        pl.semaphore_signal(
            barrier, inc=1, device_id={"horiz": peer(me, offset, count)},
            device_id_type=pl.DeviceIdType.MESH,
        )
        return carry

    lax.fori_loop(1, count, signal, 0)
    return lambda: pl.semaphore_wait(barrier, count - 1)


def block_copy(count, capacity, source, target, send, recv, offset):
    me = lax.axis_index("horiz")
    to = peer(me, offset, count)
    return pltpu.make_async_remote_copy(
        src_ref=source.at[to, pl.ds(0, capacity)],
        dst_ref=target.at[me, pl.ds(0, capacity)],
        send_sem=send.at[offset],
        recv_sem=recv.at[offset],
        device_id={"horiz": to},
        device_id_type=pl.DeviceIdType.MESH,
    )


def exchange(count, capacity, source, target, send, recv, work):
    me = lax.axis_index("horiz")

    def start(offset, carry):
        block_copy(count, capacity, source, target, send, recv, offset).start()
        return carry

    def finish(offset, carry):
        block_copy(count, capacity, source, target, send, recv, offset).wait()
        return carry

    lax.fori_loop(1, count, start, 0)
    target[me] = source[me]
    work()
    lax.fori_loop(1, count, finish, 0)


def shift_copy(count, source, target, sems, at, step):
    me = lax.axis_index("horiz")
    return pltpu.make_async_remote_copy(
        src_ref=source,
        dst_ref=target,
        send_sem=sems.at[at],
        recv_sem=sems.at[at + 1],
        device_id={"horiz": peer(me, step, count)},
        device_id_type=pl.DeviceIdType.MESH,
    )


def neighbours(field, low, high, width, group):
    rows = field.shape[0]
    tile = lax.rem(lax.broadcasted_iota(jnp.int32, field.shape, 0), group)
    lane = lax.broadcasted_iota(jnp.int32, field.shape, 1)
    east = pltpu.roll(field, 127, 1)
    following = jnp.where(
        tile == width - 1, pltpu.roll(east, width - 1, 0), pltpu.roll(east, rows - 1, 0)
    )
    east = jnp.where(lane == 127, following, east)
    west = pltpu.roll(field, 1, 1)
    before = jnp.where(tile == 0, pltpu.roll(west, rows - width + 1, 0), pltpu.roll(west, 1, 0))
    west = jnp.where(lane == 0, before, west)
    north = jnp.concatenate([low, field[: rows - group]], axis=0)
    south = jnp.concatenate([field[group:], high], axis=0)
    return north + south + east + west


def whole_kernel(
    count, width, group, hours, cell_total,
    pert, base, target, cost, coef, wet_list, wet_owner, mix_in, air_in, wind_in, chan, coupler,
    remap_src, remap_tgt, remap_weight, out,
    select, mat,
    mix, air, wind, field_a, field_b, drive, halo_low, halo_high, coef_low, coef_high, out_buf, in_buf, mixed_s,
    force_s, atmos_s, sums, got_low, got_high, stat_src, stat_got,
    send, recv, near, stat_send, stat_recv,
):
    me = lax.axis_index("horiz")
    levels, _, rows, _ = pert.shape
    slots = mix.shape[0]
    capacity = mix_in.shape[1] // count
    half = sums.shape[0] // 2
    slot_shape = (slots, 512)
    used = [0, 0, 0]

    def near_copy(source, target_ref, step):
        at = used[0]
        used[0] += 2
        return shift_copy(count, source, target_ref, near, at, step)

    def pair(down_src, down_dst, up_src, up_dst):
        copies = [near_copy(down_src, down_dst, -1), near_copy(up_src, up_dst, 1)]
        for copy in copies:
            copy.start()
        return copies

    def finish(copies):
        for copy in copies:
            copy.wait()

    def halo(ref, at, first, number):
        here = pl.ds(first + 1, number)
        there = pl.ds(first, number)
        return pair(
            ref.at[here, :, pl.ds(0, group)],
            halo_high.at[at, there],
            ref.at[here, :, pl.ds(rows - group, group)],
            halo_low.at[at, there],
        )

    def swap(values, work=lambda: None):
        at = used[1]
        used[1] += 1
        out_buf[...] = values.reshape(out_buf.shape)
        exchange(count, capacity, out_buf, in_buf.at[at], send.at[at], recv.at[at], work)
        return in_buf[at].reshape(slot_shape)

    def surface(ref):
        return jnp.concatenate([ref[1, c] for c in range(4)], axis=1)

    def add_surface(ref, added):
        for c in range(4):
            ref[1, c] = ref[1, c] + added[:, c * 128 : (c + 1) * 128]

    def remap(ref):
        at = used[2]
        used[2] += 1
        sums[...] = dot(mat[...], ref[1, 0])
        finish(
            pair(
                sums.at[pl.ds(0, half)], got_high.at[at], sums.at[pl.ds(half, half)], got_low.at[at]
            )
        )
        low = jnp.where(me > 0, got_low[at], 0.0)
        high = jnp.where(me < count - 1, got_high[at], 0.0)
        return jnp.concatenate([sums[0:half] + low, sums[half:] + high], axis=0)

    def low_of(at, l, c):
        return jnp.where(me > 0, halo_low[at, l, c], 0.0)

    def high_of(at, l, c):
        return jnp.where(me < count - 1, halo_high[at, l, c], 0.0)

    for at in range(in_buf.shape[0]):
        in_buf[at, :, capacity:] = jnp.zeros((count, PAD - capacity, 512), jnp.float32)
    all_in = greet(count)
    zeros = jnp.zeros((4, rows, 128), jnp.float32)
    for ref in (field_a, field_b):
        ref[0] = zeros
        ref[levels + 1] = zeros

    def begin(l, total):
        mine = pert[l]
        field_a[l + 1] = base[l] + mine
        return total + jnp.sum(mine * mine, axis=0)

    pp = lax.fori_loop(0, levels, begin, jnp.zeros((rows, 128), jnp.float32))
    all_in()
    waiting = halo(field_a, 0, 0, levels)
    waiting += pair(
        coef.at[pl.ds(0, group)], coef_high, coef.at[pl.ds(rows - group, group)], coef_low
    )
    ocean_rows = rows // group
    tiles = wet_list.shape[1]
    owner = wet_owner[...]
    mine = lax.broadcasted_iota(jnp.int32, (count, tiles), 0) == owner
    before = lax.broadcasted_iota(jnp.int32, (tiles, tiles), 0) < lax.broadcasted_iota(
        jnp.int32, (tiles, tiles), 1
    )
    mine = mine.astype(jnp.float32)
    earlier = jnp.sum(mine * dot(mine, before.astype(jnp.float32)), axis=0, keepdims=True)
    slot = lax.broadcasted_iota(jnp.int32, (slots, tiles), 0)
    filled = (slot // PAD == owner) & ((slot % PAD).astype(jnp.float32) == earlier)
    row = lax.broadcasted_iota(jnp.int32, (rows, tiles), 0)
    placed = (row // group * width + row % group == wet_list[...]) & (row % group < width)
    select[...] = lax.dot_general(
        filled.astype(jnp.float32), placed.astype(jnp.float32), (((1,), (1,)), ((), ())),
        precision=HIGHEST, preferred_element_type=jnp.float32,
    )
    lat = lax.broadcasted_iota(jnp.int32, mat.shape, 0)
    row = lax.broadcasted_iota(jnp.int32, mat.shape, 1)
    lat_of = jnp.where(lat % group == row % group, lat // group, -1) + (me * LAT_DEV - 1)
    lat_of = jnp.where(lat % group == row % group, lat_of, -9)
    row_of = row // group + me * ocean_rows
    table = jnp.zeros(mat.shape, jnp.float32)
    for e in range(remap_src.shape[0]):
        hit = (lat_of == remap_tgt[e]) & (row_of == remap_src[e])
        table = table + jnp.where(hit, remap_weight[e], 0.0)
    mat[...] = table
    slot = lax.broadcasted_iota(jnp.int32, (slots, count * capacity), 0)
    cell = lax.broadcasted_iota(jnp.int32, (slots, count * capacity), 1)
    rank = slot % PAD
    widen = ((slot // PAD * capacity + rank == cell) & (rank < capacity)).astype(jnp.float32)
    mix[...] = lax.dot_general(
        dot(widen, mix_in[0]), widen, (((1,), (1,)), ((), ())), precision=HIGHEST,
        preferred_element_type=jnp.float32,
    )
    for hour in range(hours):
        air[hour] = dot(widen, air_in[hour, 0])
        wind[hour] = dot(widen, wind_in[hour, 0])

    def advance(hour, old, new, first, end):
        def level(l, carry):
            xs = [old[l + 1, c] for c in range(4)]
            for c in range(4):
                pushed = jnp.tanh(sum(chan[l * 16 + c * 4 + k] * xs[k] for k in range(4)))
                drive[hour, l, c] = pushed
                around = neighbours(xs[c], low_of(hour, l, c), high_of(hour, l, c), width, group)
                new[l + 1, c] = (
                    xs[c]
                    + coef[...] * (around - 4.0 * xs[c])
                    + KAPPA_V * (old[l, c] + old[l + 2, c] - 2.0 * xs[c])
                    + TIME_STEP * pushed
                )
            return carry

        lax.fori_loop(first, end, level, 0)

    def turn(state, result, first, end):
        def level(l, carry):
            for c in range(4):
                result[l + 1, c] = cost[...] * cost[...] * (state[l + 1, c] - target[l, c])
            return carry

        lax.fori_loop(first, end, level, 0)

    old, new = field_a, field_b
    finish(waiting)
    advance(0, old, new, 0, levels)
    for hour in range(hours):
        more = hour + 1 < hours
        rest = halo(new, hour + 1, 1, levels - 1) if more else []

        def beside():
            if more:
                finish(rest)
                advance(hour + 1, new, old, 2, levels)
            else:
                turn(new, old, 1, levels)
                rest.extend(halo(old, hours, 1, levels - 1))

        got = swap(dot(select[...], surface(new)), beside)
        mixed = jnp.tanh(dot(mix[...], got))
        mixed_s[hour] = mixed
        contrast = []
        for k in range(4):
            part = got[:, k * 128 : (k + 1) * 128]
            part = air[hour] - part if k == 0 else part
            contrast.append(part + mixed[:, k * 128 : (k + 1) * 128])
        force = [
            jnp.tanh(sum(coupler[c, k] * contrast[k] for k in range(4))) for c in range(4)
        ]
        force_s[hour] = jnp.concatenate(force, axis=1)
        scaled = FLUX_RATE * wind[hour]
        back = swap(jnp.concatenate([scaled * f for f in force], axis=1))
        add_surface(new, dot_t(select[...], back))
        total = jnp.tanh(remap(new))
        atmos_s[hour] = total
        new[1, 0] = new[1, 0] + FEEDBACK * dot_t(mat[...], total)
        if more:
            top = halo(new, hour + 1, 0, 1)
            advance(hour + 1, new, old, 1, 2)
            finish(top)
            advance(hour + 1, new, old, 0, 1)
            old, new = new, old
        else:
            turn(new, old, 0, 1)

    def retreat(hour, at, old, new, first, end, carry):
        real = lax.rem(lax.broadcasted_iota(jnp.int32, (rows, 128), 0), group) < width
        factor = coef[...]

        def level(l, carry):
            pg, gg = carry
            adj = [old[l + 1, c] for c in range(4)]
            weighted = []
            for c in range(4):
                pushed = drive[hour, l, c]
                weighted.append((1.0 - pushed * pushed) * adj[c])
            for k in range(4):
                spread = factor * adj[k]
                around = neighbours(
                    spread, coef_low[...] * low_of(at, l, k), coef_high[...] * high_of(at, l, k),
                    width, group,
                )
                result = (
                    adj[k]
                    + jnp.where(real, around - 4.0 * spread, 0.0)
                    + KAPPA_V * (old[l, k] + old[l + 2, k] - 2.0 * adj[k])
                    + TIME_STEP * sum(chan[l * 16 + c * 4 + k] * weighted[c] for c in range(4))
                )
                new[l + 1, k] = result
                if hour == 0:
                    pg = pg + pert[l, k] * result
                    gg = gg + result * result
            return pg, gg

        return lax.fori_loop(first, end, level, carry)

    none = jnp.zeros((rows, 128), jnp.float32)
    sofar = [(none, none)]

    for hour in reversed(range(hours)):
        at = 2 * hours - 1 - hour
        total = FEEDBACK * remap(old)
        total = total * (1.0 - atmos_s[hour] * atmos_s[hour])
        old[1, 0] = old[1, 0] + dot_t(mat[...], total)

        def beside_adjoint():
            finish(rest)
            sofar[0] = retreat(hour, at, old, new, 2, levels, sofar[0])

        got = swap(dot(select[...], surface(old)), beside_adjoint)
        scaled = FLUX_RATE * wind[hour]
        dforce = []
        for c in range(4):
            t = force_s[hour, :, c * 128 : (c + 1) * 128]
            dforce.append(scaled * (1.0 - t * t) * got[:, c * 128 : (c + 1) * 128])
        dcontrast = [sum(coupler[c, k] * dforce[c] for c in range(4)) for k in range(4)]
        joined = jnp.concatenate(dcontrast, axis=1)
        signed = jnp.concatenate([-dcontrast[0]] + dcontrast[1:], axis=1)
        held = mixed_s[hour]
        back = swap(signed + dot_t(mix[...], (1.0 - held * held) * joined))
        add_surface(old, dot_t(select[...], back))
        top = halo(old, at, 0, 1)
        sofar[0] = retreat(hour, at, old, new, 1, 2, sofar[0])
        if hour > 0:
            rest = halo(new, at + 1, 1, levels - 1)
        finish(top)
        sofar[0] = retreat(hour, at, old, new, 0, 1, sofar[0])
        old, new = new, old
    pg, gg = sofar[0]

    for i, value in enumerate((pp, pg, gg)):
        value = value if value.ndim == 2 else jnp.sum(value, axis=0)
        stat_src[i * 8 : (i + 1) * 8] = jnp.sum(value.reshape(rows // 8, 8, 128), axis=0)

    def stat_copy(offset):
        return pltpu.make_async_remote_copy(
            src_ref=stat_src,
            dst_ref=stat_got.at[me],
            send_sem=stat_send.at[offset],
            recv_sem=stat_recv.at[offset],
            device_id={"horiz": peer(me, offset, count)},
            device_id_type=pl.DeviceIdType.MESH,
        )

    def stat_start(offset, carry):
        stat_copy(offset).start()
        return carry

    def stat_finish(offset, carry):
        stat_copy(offset).wait()
        return carry

    lax.fori_loop(1, count, stat_start, 0)
    stat_got[me] = stat_src[...]
    lax.fori_loop(1, count, stat_finish, 0)
    stats = jnp.sum(stat_got[...], axis=0)
    mean_pp, mean_pg, mean_gg = [
        jnp.sum(stats[i * 8 : (i + 1) * 8], axis=(0, 1), keepdims=True) / cell_total
        for i in range(3)
    ]
    grad_scale = lax.rsqrt(mean_gg + EPSILON)
    mean_sq = (
        mean_pp
        + 2.0 * ASCENT * grad_scale * mean_pg
        + ASCENT * ASCENT * grad_scale * grad_scale * mean_gg
    )
    norm = lax.rsqrt(mean_sq + EPSILON)

    def close(l, carry):
        for c in range(4):
            out[l, c] = (pert[l, c] + ASCENT * grad_scale * old[l + 1, c]) * norm
        return carry

    lax.fori_loop(0, levels, close, 0)


def body(
    perturbation,
    base_state,
    target_state,
    cost_weight,
    diffusivity,
    chan_mix,
    coupler_mix,
    owner_mix,
    air_temp,
    wind_speed,
    wet_list,
    wet_owner,
    remap_src,
    remap_tgt,
    remap_weight,
):
    count = lax.axis_size("horiz")
    levels, row_count, _, cells = base_state.shape
    hour_count = air_temp.shape[0]
    width = cells // 128
    group = -(-width // 8) * 8
    rows = row_count * group
    slots = count * PAD
    lat_rows = (LAT_DEV + 2) * group

    def to_tiles(field):
        pieces = field.reshape(levels, row_count, 4, width, 128).transpose(0, 2, 1, 3, 4)
        widths = ((0, 0), (0, 0), (0, 0), (0, group - width), (0, 0))
        return jnp.pad(pieces, widths).reshape(levels, 4, rows, 128)

    def column_tiles(column):
        pieces = column.reshape(row_count, width, 128)
        return jnp.pad(pieces, ((0, 0), (0, group - width), (0, 0))).reshape(rows, 128)

    f32 = jnp.float32
    rounds = 2 * hour_count
    operands = (
        to_tiles(perturbation), to_tiles(base_state), to_tiles(target_state),
        column_tiles(cost_weight), column_tiles(diffusivity), wet_list, wet_owner, owner_mix, air_temp,
        wind_speed, chan_mix.reshape(-1), coupler_mix, remap_src, remap_tgt, remap_weight,
    )
    specs = [pl.BlockSpec(memory_space=pltpu.VMEM)] * (len(operands) - 5)
    specs += [pl.BlockSpec(memory_space=pltpu.SMEM)] * 5
    result = pl.pallas_call(
        functools.partial(
            whole_kernel, count, width, group, hour_count, perturbation.size * count
        ),
        out_shape=jax.ShapeDtypeStruct((levels, 4, rows, 128), f32),
        in_specs=specs,
        out_specs=pl.BlockSpec(memory_space=pltpu.VMEM),
        scratch_shapes=[
            pltpu.VMEM((slots, rows), f32),
            pltpu.VMEM((lat_rows, rows), f32),
            pltpu.VMEM((slots, slots), f32),
            pltpu.VMEM((hour_count, slots, 128), f32),
            pltpu.VMEM((hour_count, slots, 128), f32),
            pltpu.VMEM((levels + 2, 4, rows, 128), f32),
            pltpu.VMEM((levels + 2, 4, rows, 128), f32),
            pltpu.VMEM((hour_count, levels, 4, rows, 128), f32),
            pltpu.VMEM((rounds, levels, 4, group, 128), f32),
            pltpu.VMEM((rounds, levels, 4, group, 128), f32),
            pltpu.VMEM((group, 128), f32),
            pltpu.VMEM((group, 128), f32),
            pltpu.VMEM((count, PAD, 512), f32),
            pltpu.VMEM((2 * rounds, count, PAD, 512), f32),
            pltpu.VMEM((hour_count, slots, 512), f32),
            pltpu.VMEM((hour_count, slots, 512), f32),
            pltpu.VMEM((hour_count, lat_rows, 128), f32),
            pltpu.VMEM((lat_rows, 128), f32),
            pltpu.VMEM((rounds, lat_rows // 2, 128), f32),
            pltpu.VMEM((rounds, lat_rows // 2, 128), f32),
            pltpu.VMEM((24, 128), f32),
            pltpu.VMEM((count, 24, 128), f32),
            pltpu.SemaphoreType.DMA((2 * rounds, count)),
            pltpu.SemaphoreType.DMA((2 * rounds, count)),
            pltpu.SemaphoreType.DMA((16 * rounds,)),
            pltpu.SemaphoreType.DMA((count,)),
            pltpu.SemaphoreType.DMA((count,)),
        ],
        compiler_params=pltpu.CompilerParams(
            collective_id=0, has_side_effects=True, vmem_limit_bytes=VMEM_BYTES
        ),
    )(*operands)
    pieces = result.reshape(levels, 4, row_count, group, 128)[:, :, :, :width]
    return pieces.transpose(0, 2, 1, 3, 4).reshape(perturbation.shape)


def solution(mesh):
    placed = (
        P("member", "horiz", None, None),
        P(None, "horiz", None, None),
        P(None, "horiz", None, None),
        P("horiz", None),
        P("horiz", None),
        P(),
        P(),
        P("horiz", None, None),
        P(None, "horiz", None, None),
        P(None, "horiz", None, None),
        P("horiz", None),
        P("horiz", None),
        P("horiz"),
        P("horiz"),
        P("horiz"),
    )
    return jax.shard_map(
        body,
        mesh=mesh,
        in_specs=placed,
        out_specs=P("member", "horiz", None, None),
        check_vma=False,
    )
```

```python
import functools

import jax
import jax.numpy as jnp
from jax import lax
from jax.experimental import pallas as pl
from jax.experimental.pallas import tpu as pltpu
from jax.sharding import PartitionSpec as P

LAT_DEV = 2
PAD = 8

KAPPA_V = 0.1
TIME_STEP = 0.3
FLUX_RATE = 0.05
FEEDBACK = 0.5
ASCENT = 0.5
EPSILON = 1e-06
HIGHEST = lax.Precision.HIGHEST
VMEM_BYTES = 48 * 1024 * 1024


def dot(a, b):
    return jnp.dot(a, b, precision=HIGHEST, preferred_element_type=jnp.float32)


def dot_t(a, b):
    return lax.dot_general(
        a, b, (((0,), (0,)), ((), ())), precision=HIGHEST, preferred_element_type=jnp.float32
    )


def peer(me, offset, count):
    return lax.rem(me + offset + count, count)


def greet(count):
    me = lax.axis_index("horiz")
    barrier = pltpu.get_barrier_semaphore()

    def signal(offset, carry):
        pl.semaphore_signal(
            barrier, inc=1, device_id={"horiz": peer(me, offset, count)},
            device_id_type=pl.DeviceIdType.MESH,
        )
        return carry

    lax.fori_loop(1, count, signal, 0)
    return lambda: pl.semaphore_wait(barrier, count - 1)


def block_copy(count, capacity, source, target, send, recv, offset):
    me = lax.axis_index("horiz")
    to = peer(me, offset, count)
    return pltpu.make_async_remote_copy(
        src_ref=source.at[to, pl.ds(0, capacity)],
        dst_ref=target.at[me, pl.ds(0, capacity)],
        send_sem=send.at[offset],
        recv_sem=recv.at[offset],
        device_id={"horiz": to},
        device_id_type=pl.DeviceIdType.MESH,
    )


def exchange(count, capacity, source, target, send, recv, work):
    me = lax.axis_index("horiz")

    def start(offset, carry):
        block_copy(count, capacity, source, target, send, recv, offset).start()
        return carry

    def finish(offset, carry):
        block_copy(count, capacity, source, target, send, recv, offset).wait()
        return carry

    lax.fori_loop(1, count, start, 0)
    target[me] = source[me]
    work()
    lax.fori_loop(1, count, finish, 0)


def shift_copy(count, source, target, sems, at, step):
    me = lax.axis_index("horiz")
    return pltpu.make_async_remote_copy(
        src_ref=source,
        dst_ref=target,
        send_sem=sems.at[at],
        recv_sem=sems.at[at + 1],
        device_id={"horiz": peer(me, step, count)},
        device_id_type=pl.DeviceIdType.MESH,
    )


def neighbours(field, low, high, width, group):
    rows = field.shape[0]
    tile = lax.rem(lax.broadcasted_iota(jnp.int32, field.shape, 0), group)
    lane = lax.broadcasted_iota(jnp.int32, field.shape, 1)
    east = pltpu.roll(field, 127, 1)
    following = jnp.where(
        tile == width - 1, pltpu.roll(east, width - 1, 0), pltpu.roll(east, rows - 1, 0)
    )
    east = jnp.where(lane == 127, following, east)
    west = pltpu.roll(field, 1, 1)
    before = jnp.where(tile == 0, pltpu.roll(west, rows - width + 1, 0), pltpu.roll(west, 1, 0))
    west = jnp.where(lane == 0, before, west)
    north = jnp.concatenate([low, field[: rows - group]], axis=0)
    south = jnp.concatenate([field[group:], high], axis=0)
    return north + south + east + west


def whole_kernel(
    count, width, group, hours, cell_total,
    pert, base, target, cost, coef, wet_list, wet_owner, mix_in, air_in, wind_in, chan, coupler,
    remap_src, remap_tgt, remap_weight, out,
    select, mat,
    mix, air, wind, field_a, field_b, drive, halo_low, halo_high, coef_low, coef_high, out_buf, in_buf, mixed_s,
    force_s, atmos_s, sums, got_low, got_high, stat_src, stat_got,
    send, recv, near, stat_send, stat_recv,
):
    me = lax.axis_index("horiz")
    levels, _, rows, _ = pert.shape
    slots = mix.shape[0]
    capacity = mix_in.shape[1] // count
    half = sums.shape[0] // 2
    slot_shape = (slots, 512)
    used = [0, 0, 0]

    def near_copy(source, target_ref, step):
        at = used[0]
        used[0] += 2
        return shift_copy(count, source, target_ref, near, at, step)

    def pair(down_src, down_dst, up_src, up_dst):
        copies = [near_copy(down_src, down_dst, -1), near_copy(up_src, up_dst, 1)]
        for copy in copies:
            copy.start()
        return copies

    def finish(copies):
        for copy in copies:
            copy.wait()

    def halo(ref, at, first, number):
        here = pl.ds(first + 1, number)
        there = pl.ds(first, number)
        return pair(
            ref.at[here, :, pl.ds(0, group)],
            halo_high.at[at, there],
            ref.at[here, :, pl.ds(rows - group, group)],
            halo_low.at[at, there],
        )

    def swap(values, work=lambda: None):
        at = used[1]
        used[1] += 1
        out_buf[...] = values.reshape(out_buf.shape)
        exchange(count, capacity, out_buf, in_buf.at[at], send.at[at], recv.at[at], work)
        return in_buf[at].reshape(slot_shape)

    def surface(ref):
        return jnp.concatenate([ref[1, c] for c in range(4)], axis=1)

    def add_surface(ref, added):
        for c in range(4):
            ref[1, c] = ref[1, c] + added[:, c * 128 : (c + 1) * 128]

    def remap(ref):
        at = used[2]
        used[2] += 1
        sums[...] = dot(mat[...], ref[1, 0])
        finish(
            pair(
                sums.at[pl.ds(0, half)], got_high.at[at], sums.at[pl.ds(half, half)], got_low.at[at]
            )
        )
        low = jnp.where(me > 0, got_low[at], 0.0)
        high = jnp.where(me < count - 1, got_high[at], 0.0)
        return jnp.concatenate([sums[0:half] + low, sums[half:] + high], axis=0)

    def low_of(at, l, c):
        return jnp.where(me > 0, halo_low[at, l, c], 0.0)

    def high_of(at, l, c):
        return jnp.where(me < count - 1, halo_high[at, l, c], 0.0)

    for at in range(in_buf.shape[0]):
        in_buf[at, :, capacity:] = jnp.zeros((count, PAD - capacity, 512), jnp.float32)
    all_in = greet(count)
    zeros = jnp.zeros((4, rows, 128), jnp.float32)
    for ref in (field_a, field_b):
        ref[0] = zeros
        ref[levels + 1] = zeros

    def begin(l, total):
        mine = pert[l]
        field_a[l + 1] = base[l] + mine
        return total + jnp.sum(mine * mine, axis=0)

    pp = lax.fori_loop(0, levels, begin, jnp.zeros((rows, 128), jnp.float32))
    all_in()
    waiting = halo(field_a, 0, 0, levels)
    waiting += pair(
        coef.at[pl.ds(0, group)], coef_high, coef.at[pl.ds(rows - group, group)], coef_low
    )
    ocean_rows = rows // group
    tiles = wet_list.shape[1]
    owner = wet_owner[...]
    mine = lax.broadcasted_iota(jnp.int32, (count, tiles), 0) == owner
    before = lax.broadcasted_iota(jnp.int32, (tiles, tiles), 0) < lax.broadcasted_iota(
        jnp.int32, (tiles, tiles), 1
    )
    mine = mine.astype(jnp.float32)
    earlier = jnp.sum(mine * dot(mine, before.astype(jnp.float32)), axis=0, keepdims=True)
    slot = lax.broadcasted_iota(jnp.int32, (slots, tiles), 0)
    filled = (slot // PAD == owner) & ((slot % PAD).astype(jnp.float32) == earlier)
    row = lax.broadcasted_iota(jnp.int32, (rows, tiles), 0)
    placed = (row // group * width + row % group == wet_list[...]) & (row % group < width)
    select[...] = lax.dot_general(
        filled.astype(jnp.float32), placed.astype(jnp.float32), (((1,), (1,)), ((), ())),
        precision=HIGHEST, preferred_element_type=jnp.float32,
    )
    lat = lax.broadcasted_iota(jnp.int32, mat.shape, 0)
    row = lax.broadcasted_iota(jnp.int32, mat.shape, 1)
    lat_of = jnp.where(lat % group == row % group, lat // group, -1) + (me * LAT_DEV - 1)
    lat_of = jnp.where(lat % group == row % group, lat_of, -9)
    row_of = row // group + me * ocean_rows
    table = jnp.zeros(mat.shape, jnp.float32)
    for e in range(remap_src.shape[0]):
        hit = (lat_of == remap_tgt[e]) & (row_of == remap_src[e])
        table = table + jnp.where(hit, remap_weight[e], 0.0)
    mat[...] = table
    slot = lax.broadcasted_iota(jnp.int32, (slots, count * capacity), 0)
    cell = lax.broadcasted_iota(jnp.int32, (slots, count * capacity), 1)
    rank = slot % PAD
    widen = ((slot // PAD * capacity + rank == cell) & (rank < capacity)).astype(jnp.float32)
    mix[...] = lax.dot_general(
        dot(widen, mix_in[0]), widen, (((1,), (1,)), ((), ())), precision=HIGHEST,
        preferred_element_type=jnp.float32,
    )
    for hour in range(hours):
        air[hour] = dot(widen, air_in[hour, 0])
        wind[hour] = dot(widen, wind_in[hour, 0])

    def advance(hour, old, new, first, end):
        def level(l, carry):
            xs = [old[l + 1, c] for c in range(4)]
            for c in range(4):
                pushed = jnp.tanh(sum(chan[l * 16 + c * 4 + k] * xs[k] for k in range(4)))
                drive[hour, l, c] = pushed
                around = neighbours(xs[c], low_of(hour, l, c), high_of(hour, l, c), width, group)
                new[l + 1, c] = (
                    xs[c]
                    + coef[...] * (around - 4.0 * xs[c])
                    + KAPPA_V * (old[l, c] + old[l + 2, c] - 2.0 * xs[c])
                    + TIME_STEP * pushed
                )
            return carry

        lax.fori_loop(first, end, level, 0)

    def turn(state, result, first, end):
        def level(l, carry):
            for c in range(4):
                result[l + 1, c] = cost[...] * cost[...] * (state[l + 1, c] - target[l, c])
            return carry

        lax.fori_loop(first, end, level, 0)

    old, new = field_a, field_b
    finish(waiting)
    advance(0, old, new, 0, levels)
    for hour in range(hours):
        more = hour + 1 < hours
        rest = []

        def beside_first():
            if more:
                rest.extend(halo(new, hour + 1, 1, levels - 1))
            else:
                turn(new, old, 1, levels)
                rest.extend(halo(old, hours, 1, levels - 1))

        def beside_second():
            if more:
                finish(rest)
                advance(hour + 1, new, old, 2, levels)

        got = swap(dot(select[...], surface(new)), beside_first)
        mixed = jnp.tanh(dot(mix[...], got))
        mixed_s[hour] = mixed
        contrast = []
        for k in range(4):
            part = got[:, k * 128 : (k + 1) * 128]
            part = air[hour] - part if k == 0 else part
            contrast.append(part + mixed[:, k * 128 : (k + 1) * 128])
        force = [
            jnp.tanh(sum(coupler[c, k] * contrast[k] for k in range(4))) for c in range(4)
        ]
        force_s[hour] = jnp.concatenate(force, axis=1)
        scaled = FLUX_RATE * wind[hour]
        back = swap(jnp.concatenate([scaled * f for f in force], axis=1), beside_second)
        add_surface(new, dot_t(select[...], back))
        total = jnp.tanh(remap(new))
        atmos_s[hour] = total
        new[1, 0] = new[1, 0] + FEEDBACK * dot_t(mat[...], total)
        if more:
            top = halo(new, hour + 1, 0, 1)
            advance(hour + 1, new, old, 1, 2)
            finish(top)
            advance(hour + 1, new, old, 0, 1)
            old, new = new, old
        else:
            turn(new, old, 0, 1)

    def retreat(hour, at, old, new, first, end, carry):
        real = lax.rem(lax.broadcasted_iota(jnp.int32, (rows, 128), 0), group) < width
        factor = coef[...]

        def level(l, carry):
            pg, gg = carry
            adj = [old[l + 1, c] for c in range(4)]
            weighted = []
            for c in range(4):
                pushed = drive[hour, l, c]
                weighted.append((1.0 - pushed * pushed) * adj[c])
            for k in range(4):
                spread = factor * adj[k]
                around = neighbours(
                    spread, coef_low[...] * low_of(at, l, k), coef_high[...] * high_of(at, l, k),
                    width, group,
                )
                result = (
                    adj[k]
                    + jnp.where(real, around - 4.0 * spread, 0.0)
                    + KAPPA_V * (old[l, k] + old[l + 2, k] - 2.0 * adj[k])
                    + TIME_STEP * sum(chan[l * 16 + c * 4 + k] * weighted[c] for c in range(4))
                )
                new[l + 1, k] = result
                if hour == 0:
                    pg = pg + pert[l, k] * result
                    gg = gg + result * result
            return pg, gg

        return lax.fori_loop(first, end, level, carry)

    none = jnp.zeros((rows, 128), jnp.float32)
    sofar = [(none, none)]

    for hour in reversed(range(hours)):
        at = 2 * hours - 1 - hour
        total = FEEDBACK * remap(old)
        total = total * (1.0 - atmos_s[hour] * atmos_s[hour])
        old[1, 0] = old[1, 0] + dot_t(mat[...], total)

        def start_rest():
            if hour + 1 < hours:
                rest.extend(halo(old, at, 1, levels - 1))

        def beside_adjoint():
            finish(rest)
            sofar[0] = retreat(hour, at, old, new, 2, levels, sofar[0])

        got = swap(dot(select[...], surface(old)), start_rest)
        scaled = FLUX_RATE * wind[hour]
        dforce = []
        for c in range(4):
            t = force_s[hour, :, c * 128 : (c + 1) * 128]
            dforce.append(scaled * (1.0 - t * t) * got[:, c * 128 : (c + 1) * 128])
        dcontrast = [sum(coupler[c, k] * dforce[c] for c in range(4)) for k in range(4)]
        joined = jnp.concatenate(dcontrast, axis=1)
        signed = jnp.concatenate([-dcontrast[0]] + dcontrast[1:], axis=1)
        held = mixed_s[hour]
        back = swap(signed + dot_t(mix[...], (1.0 - held * held) * joined), beside_adjoint)
        add_surface(old, dot_t(select[...], back))
        top = halo(old, at, 0, 1)
        sofar[0] = retreat(hour, at, old, new, 1, 2, sofar[0])
        rest = []
        finish(top)
        sofar[0] = retreat(hour, at, old, new, 0, 1, sofar[0])
        old, new = new, old
    pg, gg = sofar[0]

    for i, value in enumerate((pp, pg, gg)):
        value = value if value.ndim == 2 else jnp.sum(value, axis=0)
        stat_src[i * 8 : (i + 1) * 8] = jnp.sum(value.reshape(rows // 8, 8, 128), axis=0)

    def stat_copy(offset):
        return pltpu.make_async_remote_copy(
            src_ref=stat_src,
            dst_ref=stat_got.at[me],
            send_sem=stat_send.at[offset],
            recv_sem=stat_recv.at[offset],
            device_id={"horiz": peer(me, offset, count)},
            device_id_type=pl.DeviceIdType.MESH,
        )

    def stat_start(offset, carry):
        stat_copy(offset).start()
        return carry

    def stat_finish(offset, carry):
        stat_copy(offset).wait()
        return carry

    lax.fori_loop(1, count, stat_start, 0)
    stat_got[me] = stat_src[...]
    lax.fori_loop(1, count, stat_finish, 0)
    stats = jnp.sum(stat_got[...], axis=0)
    mean_pp, mean_pg, mean_gg = [
        jnp.sum(stats[i * 8 : (i + 1) * 8], axis=(0, 1), keepdims=True) / cell_total
        for i in range(3)
    ]
    grad_scale = lax.rsqrt(mean_gg + EPSILON)
    mean_sq = (
        mean_pp
        + 2.0 * ASCENT * grad_scale * mean_pg
        + ASCENT * ASCENT * grad_scale * grad_scale * mean_gg
    )
    norm = lax.rsqrt(mean_sq + EPSILON)

    def close(l, carry):
        for c in range(4):
            out[l, c] = (pert[l, c] + ASCENT * grad_scale * old[l + 1, c]) * norm
        return carry

    lax.fori_loop(0, levels, close, 0)


def body(
    perturbation,
    base_state,
    target_state,
    cost_weight,
    diffusivity,
    chan_mix,
    coupler_mix,
    owner_mix,
    air_temp,
    wind_speed,
    wet_list,
    wet_owner,
    remap_src,
    remap_tgt,
    remap_weight,
):
    count = lax.axis_size("horiz")
    levels, row_count, _, cells = base_state.shape
    hour_count = air_temp.shape[0]
    width = cells // 128
    group = -(-width // 8) * 8
    rows = row_count * group
    slots = count * PAD
    lat_rows = (LAT_DEV + 2) * group

    def to_tiles(field):
        pieces = field.reshape(levels, row_count, 4, width, 128).transpose(0, 2, 1, 3, 4)
        widths = ((0, 0), (0, 0), (0, 0), (0, group - width), (0, 0))
        return jnp.pad(pieces, widths).reshape(levels, 4, rows, 128)

    def column_tiles(column):
        pieces = column.reshape(row_count, width, 128)
        return jnp.pad(pieces, ((0, 0), (0, group - width), (0, 0))).reshape(rows, 128)

    f32 = jnp.float32
    rounds = 2 * hour_count
    operands = (
        to_tiles(perturbation), to_tiles(base_state), to_tiles(target_state),
        column_tiles(cost_weight), column_tiles(diffusivity), wet_list, wet_owner, owner_mix, air_temp,
        wind_speed, chan_mix.reshape(-1), coupler_mix, remap_src, remap_tgt, remap_weight,
    )
    specs = [pl.BlockSpec(memory_space=pltpu.VMEM)] * (len(operands) - 5)
    specs += [pl.BlockSpec(memory_space=pltpu.SMEM)] * 5
    result = pl.pallas_call(
        functools.partial(
            whole_kernel, count, width, group, hour_count, perturbation.size * count
        ),
        out_shape=jax.ShapeDtypeStruct((levels, 4, rows, 128), f32),
        in_specs=specs,
        out_specs=pl.BlockSpec(memory_space=pltpu.VMEM),
        scratch_shapes=[
            pltpu.VMEM((slots, rows), f32),
            pltpu.VMEM((lat_rows, rows), f32),
            pltpu.VMEM((slots, slots), f32),
            pltpu.VMEM((hour_count, slots, 128), f32),
            pltpu.VMEM((hour_count, slots, 128), f32),
            pltpu.VMEM((levels + 2, 4, rows, 128), f32),
            pltpu.VMEM((levels + 2, 4, rows, 128), f32),
            pltpu.VMEM((hour_count, levels, 4, rows, 128), f32),
            pltpu.VMEM((rounds, levels, 4, group, 128), f32),
            pltpu.VMEM((rounds, levels, 4, group, 128), f32),
            pltpu.VMEM((group, 128), f32),
            pltpu.VMEM((group, 128), f32),
            pltpu.VMEM((count, PAD, 512), f32),
            pltpu.VMEM((2 * rounds, count, PAD, 512), f32),
            pltpu.VMEM((hour_count, slots, 512), f32),
            pltpu.VMEM((hour_count, slots, 512), f32),
            pltpu.VMEM((hour_count, lat_rows, 128), f32),
            pltpu.VMEM((lat_rows, 128), f32),
            pltpu.VMEM((rounds, lat_rows // 2, 128), f32),
            pltpu.VMEM((rounds, lat_rows // 2, 128), f32),
            pltpu.VMEM((24, 128), f32),
            pltpu.VMEM((count, 24, 128), f32),
            pltpu.SemaphoreType.DMA((2 * rounds, count)),
            pltpu.SemaphoreType.DMA((2 * rounds, count)),
            pltpu.SemaphoreType.DMA((16 * rounds,)),
            pltpu.SemaphoreType.DMA((count,)),
            pltpu.SemaphoreType.DMA((count,)),
        ],
        compiler_params=pltpu.CompilerParams(
            collective_id=0, has_side_effects=True, vmem_limit_bytes=VMEM_BYTES
        ),
    )(*operands)
    pieces = result.reshape(levels, 4, row_count, group, 128)[:, :, :, :width]
    return pieces.transpose(0, 2, 1, 3, 4).reshape(perturbation.shape)


def solution(mesh):
    placed = (
        P("member", "horiz", None, None),
        P(None, "horiz", None, None),
        P(None, "horiz", None, None),
        P("horiz", None),
        P("horiz", None),
        P(),
        P(),
        P("horiz", None, None),
        P(None, "horiz", None, None),
        P(None, "horiz", None, None),
        P("horiz", None),
        P("horiz", None),
        P("horiz"),
        P("horiz"),
        P("horiz"),
    )
    return jax.shard_map(
        body,
        mesh=mesh,
        in_specs=placed,
        out_specs=P("member", "horiz", None, None),
        check_vma=False,
    )
```
